128 devices in a mesh: depth: 4 (over y), row: 8 (over x, z_hi), column: 4 (over z_lo, core).
Axes of the slice: x: 4, y: 4, z: 4 (z_hi: 2, z_lo: 2; z = z_hi * 2 + z_lo), core: 2. Of those that a mesh axis runs over, the one named last changes fastest.
Arguments:
- vir_irrep: int32 [1024], replicated, may hold values from 0 to 7, as said below
- occ_irrep: int32 [150], replicated, may hold values from 0 to 7, as said below
- allowed: int32 [8, 8, 8], replicated, may hold values 0 or 1
- pair_list: int32 [32, 2], replicated, may hold values from 0 to 149, as said below
- occ_energy: float32 [150], replicated, may hold values from -2 to -0.3
- vir_energy: float32 [1024], replicated, may hold values from 0.1 to 3
- ladder_amp: float32 [32, 1024, 256], P(None, 'depth', ('row', 'column')), may hold values from -6 to 6
- int_slab: float32 [8, 256, 1024, 256], P('row', 'column', 'depth'), may hold values from -0.015625 to 0.015625
- cycle_amp: float32 [32, 8, 153600], P(None, None, ('depth', 'row')), may hold values from -6 to 6
- cycle_int: float32 [153600, 4, 256], P(('depth', 'row'), None, 'column'), may hold values from -0.015625 to 0.015625
Outputs:
- new_amp: float32 [8, 32, 256], P('row', 'depth', 'column')
The draws below stay inside these ranges and needn't reach their ends.
Inputs may be any that keep to these rules, and one draw needn't show every extreme that they name: `vir_irrep`: Nondecreasing; every irrep labels one run of between a quarter of 256 and 256 orbitals, and one run has exactly 256. `occ_irrep`: every irrep labels at least one occupied orbital. `pair_list`: column 0 is an occupied orbital i, column 1 an occupied orbital j below 4; occ_irrep[i] XOR occ_irrep[j] is the same for all pairs.
All inputs are finite; a program needn't handle non-finite values.
Results may differ from the reference program's by a relative error of at most 0.0003.
Values sent between devices are 32-bit elements; how exact they have to be, the bound alone decides.
No kernel may reach another device: no remote copies, remote signals or barrier semaphores. Data moves between devices by JAX's collectives and lax.ppermute only.
A program may use at most 128 MiB of HBM per device.

```python
import jax
import jax.numpy as jnp
from jax import lax

NV = 1024
OCCUPIED_COUNT = 150
BB = 256
NIRR = 8
JW = 4
NP = 32
A_WIN = 8
KC = 153600


def occupied_labels(key):
    key = jax.random.fold_in(key, 11)
    first_key, second_key = jax.random.split(key)
    fixed = jax.random.permutation(first_key, 8).astype(jnp.int32)
    others = jax.random.randint(second_key, (OCCUPIED_COUNT,), 0, 8).astype(jnp.int32)
    target_positions = jnp.arange(OCCUPIED_COUNT, dtype=jnp.int32)
    return jnp.where(target_positions < 8, fixed[jnp.minimum(target_positions, 7)], others)


def draw_vir_irrep(key, part):
    key = jax.random.fold_in(key, 3)
    first_key, second_key = jax.random.split(key)
    order = jax.random.permutation(first_key, 8)
    moves = jax.random.randint(second_key, (2,), 0, BB // 4 + 1).astype(jnp.int32)
    half = BB // 2
    values = jnp.stack([jnp.int32(BB), jnp.int32(BB // 4), jnp.int32(BB // 4), half + moves[0], half - moves[0], half + moves[1], half - moves[1], jnp.int32(half)]).astype(jnp.int32)
    sizes = jnp.zeros((8,), jnp.int32).at[order].set(values)
    bounds = jnp.cumsum(sizes)
    target_positions = jnp.arange(NV, dtype=jnp.int32)
    return jnp.sum((target_positions[:, None] >= bounds[None, :]).astype(jnp.int32), axis=1)


def draw_occ_irrep(key, part):
    symmetry_labels = occupied_labels(key)
    return symmetry_labels


def draw_pair_list(key, part):
    symmetry_labels = occupied_labels(key)
    key = jax.random.fold_in(key, 7)
    second_key = jax.random.fold_in(key, 1)
    third_key = jax.random.fold_in(key, 2)
    second = jax.random.randint(second_key, (NP,), 0, JW).astype(jnp.int32)
    symmetry = jnp.bitwise_xor(symmetry_labels[OCCUPIED_COUNT - 1], symmetry_labels[second[0]])
    requested_rows = jnp.bitwise_xor(symmetry_labels[second], symmetry)
    random_jitter = jax.random.randint(third_key, (NP, OCCUPIED_COUNT), 0, OCCUPIED_COUNT).astype(jnp.int32)
    target_positions = jnp.arange(OCCUPIED_COUNT, dtype=jnp.int32)
    virtual_rows = jnp.arange(NP, dtype=jnp.int32)
    extra_reward = ((virtual_rows[:, None] == 0) & (target_positions[None, :] == OCCUPIED_COUNT - 1)).astype(jnp.int32) * (OCCUPIED_COUNT * OCCUPIED_COUNT * OCCUPIED_COUNT)
    merit_value = (symmetry_labels[None, :] == requested_rows[:, None]).astype(jnp.int32) * (OCCUPIED_COUNT * OCCUPIED_COUNT) + random_jitter * OCCUPIED_COUNT + target_positions[None, :] + extra_reward
    first = jnp.argmax(merit_value, axis=1).astype(jnp.int32)
    return jnp.stack([first, second], axis=1)


def touch_ends(drawn, rng, smallest, top_value):
    extent = drawn.shape
    place = [jax.random.randint(jax.random.fold_in(rng, axis), (), 0, extent[axis]) for axis in range(len(extent))]
    drawn = drawn.at[tuple(place)].set(smallest)
    longest = extent.index(max(extent))
    place[longest] = (place[longest] + 1) % extent[longest]
    return drawn.at[tuple(place)].set(top_value)


def block_levels(own_key, extent, cuts, low, high):
    level = 1.0
    for position, shards_of in cuts:
        heights = jax.random.uniform(jax.random.fold_in(jax.random.fold_in(own_key, 6), position), (shards_of,), jnp.float32, low / len(cuts), high / len(cuts))
        level = level * jnp.repeat(jnp.exp(heights), extent[position] // shards_of).reshape((-1,) + (1,) * (len(extent) - 1 - position))
    return level


def normal_values(own_key, shape, scale, limit, pieces=(), kind=jnp.bfloat16):
    array = scale * jax.random.normal(own_key, shape, jnp.float32)
    if pieces:
        array = array * block_levels(own_key, shape, pieces, -0.22, 0.18)
    return jnp.clip(array, -limit, limit).astype(kind)


def setup_inputs(seed: int = 0) -> dict:
    splits = jax.random.split(jax.random.key(seed), 11)
    vir_irrep = draw_vir_irrep(jax.random.fold_in(splits[10], 71), 0)
    occ_irrep = draw_occ_irrep(jax.random.fold_in(splits[10], 71), 0)
    allowed = touch_ends((jax.random.randint(splits[2], (NIRR, NIRR, NIRR), 0, 4) < 3).astype(jnp.int32), jax.random.fold_in(splits[2], 1), 0, 1)
    pair_list = draw_pair_list(jax.random.fold_in(splits[10], 71), 0)
    occ_energy = jnp.clip(jax.random.uniform(splits[4], (OCCUPIED_COUNT,), jnp.float32, -2.0, -0.3), -2.0, -0.3)
    vir_energy = jnp.clip(jax.random.uniform(splits[5], (NV,), jnp.float32, 0.1, 3.0), 0.1, 3.0)
    ladder_amp = normal_values(splits[6], (NP, NV, BB), 1.0, 6.0, ((1, 4), (2, 32)), jnp.float32)
    int_slab = normal_values(splits[7], (A_WIN, BB, NV, BB), (NV * BB // 2) ** -0.5, 0.015625, ((0, 8), (1, 4), (2, 4)), jnp.float32)
    cycle_amp = normal_values(splits[8], (NP, A_WIN, KC), 1.0, 6.0, ((2, 32),), jnp.float32)
    cycle_int = normal_values(splits[9], (KC, JW, BB), KC ** -0.5, 0.015625, ((0, 32), (2, 4)), jnp.float32)
    return {"vir_irrep": vir_irrep, "occ_irrep": occ_irrep, "allowed": allowed, "pair_list": pair_list, "occ_energy": occ_energy, "vir_energy": vir_energy, "ladder_amp": ladder_amp, "int_slab": int_slab, "cycle_amp": cycle_amp, "cycle_int": cycle_int}


def lookup(table, index):
    hits = (index[..., None] == jnp.arange(table.shape[0], dtype=jnp.int32)).astype(table.dtype)
    return jnp.sum(hits * table, axis=-1)


def reference(vir_irrep, occ_irrep, allowed, pair_list, occ_energy, vir_energy, ladder_amp, int_slab, cycle_amp, cycle_int):
    groups = jnp.arange(NIRR, dtype=jnp.int32)
    pair_irrep = jnp.bitwise_xor(lookup(occ_irrep, pair_list[0, 0]), lookup(occ_irrep, pair_list[0, 1]))
    counts = jnp.sum((vir_irrep[None, :] == groups[:, None]).astype(jnp.int32), axis=1)
    starts = jnp.sum((vir_irrep[None, :] < groups[:, None]).astype(jnp.int32), axis=1)
    a_orb = jnp.arange(A_WIN, dtype=jnp.int32) * (NV // A_WIN)
    a_irrep = lookup(vir_irrep, a_orb)
    b_irrep = jnp.bitwise_xor(a_irrep, pair_irrep)
    slots = jnp.arange(BB, dtype=jnp.int32)
    b_orb = lookup(starts, b_irrep)[:, None] + slots[None, :]
    row_live = slots[None, :] < lookup(counts, b_irrep)[:, None]
    d_count = lookup(counts, jnp.bitwise_xor(vir_irrep, pair_irrep))
    live = (slots[None, :] < d_count[:, None]).astype(jnp.float32)
    pattern = allowed.astype(jnp.float32)
    sel_a = (a_irrep[:, None] == groups[None, :]).astype(jnp.float32)
    sel_b = (b_irrep[:, None] == groups[None, :]).astype(jnp.float32)
    kept_rows = jnp.einsum("xyg,ax,ay->ag", pattern, sel_a, sel_b, precision=lax.Precision.HIGHEST)
    sel_c = (vir_irrep[:, None] == groups[None, :]).astype(jnp.float32)
    allow = jnp.dot(kept_rows, sel_c.T, precision=lax.Precision.HIGHEST, preferred_element_type=jnp.float32)

    def ladder_row(index):
        weights = ladder_amp * (live * allow[index][:, None])[None]
        block = int_slab[index]
        return jnp.dot(weights.reshape(NP, NV * BB), block.reshape(BB, NV * BB).T, precision=lax.Precision.HIGHEST, preferred_element_type=jnp.float32)

    ladder = lax.map(ladder_row, jnp.arange(A_WIN, dtype=jnp.int32))

    def cycle_row(index):
        column = lax.dynamic_index_in_dim(cycle_int, pair_list[index, 1], 1, keepdims=False)
        return jnp.dot(cycle_amp[index], column, precision=lax.Precision.HIGHEST, preferred_element_type=jnp.float32)

    cycle = jnp.transpose(lax.map(cycle_row, jnp.arange(NP, dtype=jnp.int32)), (1, 0, 2))
    eps_i = lookup(occ_energy, pair_list[:, 0])
    eps_j = lookup(occ_energy, pair_list[:, 1])
    eps_a = lookup(vir_energy, a_orb)
    eps_b = lookup(vir_energy, b_orb)
    denom = (eps_i + eps_j)[None, :, None] - eps_a[:, None, None] - eps_b[:, None, :]
    return jnp.where(row_live[:, None, :], (ladder + cycle) / denom, jnp.float32(0.0))
```

```python
import functools

import jax
import jax.numpy as jnp
from jax import lax
from jax.experimental import pallas as pl
from jax.experimental.pallas import tpu as pltpu
from jax.sharding import PartitionSpec as P

AXES = ("depth", "row", "column")
F32 = jnp.float32
BF16 = jnp.bfloat16
MIB = 1 << 20


def pairs_of(core0, core1):
    out = []
    for y in range(4):
        for x in range(4):
            for z in range(4):
                for k in range(2):
                    ty, tx, tz, tk = (core1 if k else core0)(y, x, z, k)
                    out.append((y * 32 + x * 8 + z * 2 + k, (ty % 4) * 32 + (tx % 4) * 8 + (tz % 4) * 2 + tk % 2))
    return out


def along_x(n):
    return lambda y, x, z, k: (y, x + n, z, k)


def along_y(n):
    return lambda y, x, z, k: (y + n, x, z, k)


def along_z(n):
    return lambda y, x, z, k: (y, x, z + n, k)


def other_core(y, x, z, k):
    return (y, x, z, k + 1)


FIRST = {n: pairs_of(along_x(n), along_z(n)) for n in (1, -1, 2)}
SECOND = {n: pairs_of(along_z(n), along_x(n)) for n in (1, -1, 2)}
ALONG_X = {n: pairs_of(along_x(n), along_x(n)) for n in (1, -1, 2)}
ALONG_Y = {n: pairs_of(along_y(n), along_y(n)) for n in (1, -1, 2)}
Z_ACROSS = pairs_of(along_z(2), along_z(2))
SWAP = pairs_of(other_core, other_core)


def send(value, pairs):
    return lax.ppermute(value, AXES, pairs)


def smem():
    return pl.BlockSpec(memory_space=pltpu.SMEM)


def vmem():
    return pl.BlockSpec(memory_space=pltpu.VMEM)


def hbm():
    return pl.BlockSpec(memory_space=pl.ANY)


def relayout_body(amp_ref, out_ref, turned):
    pairs, slots, cells = amp_ref.shape
    groups = cells // 8
    for t in range(slots):
        turned[t] = amp_ref[:, t, :].T
    for t in range(slots):
        pieces = [turned[t, pl.ds(j, groups, stride=8), :] for j in range(8)]
        out_ref[:, t, :] = jnp.concatenate(pieces, axis=1)


def relayout(amp):
    pairs, slots, cells = amp.shape
    return pl.pallas_call(
        relayout_body,
        out_shape=jax.ShapeDtypeStruct((cells // 8, slots, 8 * pairs), F32),
        in_specs=[vmem()],
        out_specs=vmem(),
        scratch_shapes=[pltpu.VMEM((slots, cells, pairs), F32)],
        cost_estimate=pl.CostEstimate(flops=1000, bytes_accessed=2 * MIB, transcendentals=0),
    )(amp)


def stack_body(place, b0, b1, b2, b3, q0, q1, q2, q3, sems):
    core = place[3]
    own = jnp.where(core == 0, place[1], place[2])
    copies = []
    for n, (source, shift) in enumerate(((b0, 0), (b1, 3), (b2, 1), (b3, 2))):
        at = lax.rem(own + shift, 4)
        for i, q in enumerate((q0, q1, q2, q3)):
            copies.append(pltpu.make_async_copy(source.at[pl.ds(8 * i, 8)], q.at[:, at], sems.at[n, i]))
    for c in copies:
        c.start()
    for c in copies:
        c.wait()


def stack(place, blocks):
    groups, slots, lanes = blocks[0].shape
    quarter = jax.ShapeDtypeStruct((groups // 4, 4, slots, lanes), F32)
    return pl.pallas_call(
        stack_body,
        out_shape=(quarter,) * 4,
        in_specs=[smem()] + [hbm()] * 4,
        out_specs=(hbm(),) * 4,
        scratch_shapes=[pltpu.SemaphoreType.DMA((4, 4))],
        cost_estimate=pl.CostEstimate(flops=1000, bytes_accessed=4 * MIB, transcendentals=0),
    )(place, *blocks)


def dot_nt(a, b):
    return lax.dot_general(a, b, (((1,), (1,)), ((), ())), preferred_element_type=F32)


def split(value):
    high = value.astype(BF16)
    return high, (value - high.astype(F32)).astype(BF16)


def cycle_body(place, amp_ref, int_ref, choice_ref, o0, o1, o2, o3, int_high, int_low, by_row):
    step = pl.program_id(0)
    width = int_ref.shape[1]
    window = int_ref.shape[0]

    @pl.when(step == 0)
    def _():
        for j in range(window):
            high, low = split(int_ref[j])
            int_high[pl.ds(j * width, width), :] = high
            int_low[pl.ds(j * width, width), :] = low

    pairs, rows, depth = amp_ref.shape
    high, low = split(amp_ref[...].reshape(pairs * rows, depth))
    full = dot_nt(high, int_high[...]) + dot_nt(high, int_low[...]) + dot_nt(low, int_high[...])
    total = jnp.zeros((pairs * rows, width), F32)
    for j in range(window):
        pick = choice_ref[:, j : j + 1]
        total = total + pick * full[:, j * width : (j + 1) * width]
    by_row[pl.ds(step * pairs, pairs)] = total.reshape(pairs, rows, width)

    @pl.when(step == pl.num_programs(0) - 1)
    def _():
        x = place[1]
        for out, shift in ((o0, 0), (o1, 1), (o2, 3), (o3, 2)):
            at = lax.rem(x + shift, 4)
            for other in range(4):

                @pl.when(at == other)
                def _(out=out, other=other):
                    for h in range(2):
                        out[h] = by_row[:, 2 * other + h, :]


def cycle(place, amp, ints, choice):
    pairs, rows, depth = amp.shape
    window, width, _ = ints.shape
    steps = 4
    block = pairs // steps
    part = jax.ShapeDtypeStruct((2, pairs, width), F32)
    whole = pl.BlockSpec((2, pairs, width), lambda i: (0, 0, 0))
    return pl.pallas_call(
        cycle_body,
        grid=(steps,),
        out_shape=(part,) * 4,
        in_specs=[
            smem(),
            pl.BlockSpec((block, rows, depth), lambda i: (i, 0, 0)),
            pl.BlockSpec((window, width, depth), lambda i: (0, 0, 0)),
            pl.BlockSpec((block * rows, window), lambda i: (i, 0)),
        ],
        out_specs=(whole,) * 4,
        scratch_shapes=[
            pltpu.VMEM((window * width, depth), BF16),
            pltpu.VMEM((window * width, depth), BF16),
            pltpu.VMEM((pairs, rows, width), F32),
        ],
        compiler_params=pltpu.CompilerParams(vmem_limit_bytes=40 * MIB),
        cost_estimate=pl.CostEstimate(flops=2 * 3 * 256 * 256 * 4800, bytes_accessed=10 * MIB, transcendentals=0),
    )(place, amp, ints, choice)


def join_body(place, a0, a1, a2, a3, keep, away):
    half = lax.div(place[2], 2)
    total = a0[...] + a1[...] + a2[...] + a3[...]
    keep[...] = jnp.where(half == 0, total[0], total[1])
    away[...] = jnp.where(half == 0, total[1], total[0])


def join(place, parts):
    one = jax.ShapeDtypeStruct(parts[0].shape[1:], F32)
    return pl.pallas_call(
        join_body,
        out_shape=(one, one),
        in_specs=[smem()] + [vmem()] * 4,
        out_specs=(vmem(), vmem()),
        cost_estimate=pl.CostEstimate(flops=1000, bytes_accessed=100000, transcendentals=0),
    )(place, *parts)


def labels_body(place, vir, occ, allowed, pair_list, occ_e, vir_e, vir_tile, cell_irrep, bound, denom, live):
    y, x, z, core = place[0], place[1], place[2], place[3]
    row = x * 2 + lax.div(z, 2)
    column = lax.rem(z, 2) * 2 + core
    groups = 8
    pair_irrep = jnp.bitwise_xor(occ[pair_list[0, 0]], occ[pair_list[0, 1]])
    a_orb = row * 128
    ga = vir[a_orb]
    gb = jnp.bitwise_xor(ga, pair_irrep)
    tile = vir_tile[...]
    count_b = jnp.int32(0)
    start_b = jnp.int32(0)
    below = jnp.int32(0)
    irrep = cell_irrep[...]
    limit = jnp.zeros(irrep.shape, jnp.int32)
    for g in range(groups):
        count = jnp.sum((tile == g).astype(jnp.int32))
        count_b = jnp.where(gb == g, count, count_b)
        start_b = jnp.where(gb == g, below, start_b)
        below = below + count
        partner = jnp.bitwise_xor(pair_irrep, g)
        kept = allowed[ga, gb, partner]
        limit = jnp.where(irrep == partner, count * kept, limit)
    lanes = bound.shape[1] // 8
    bound[...] = jnp.concatenate(
        [jnp.broadcast_to(limit[:, j : j + 1], (bound.shape[0], lanes)) for j in range(8)], axis=1
    )
    own, width = denom.shape
    slot = column * width + lax.broadcasted_iota(jnp.int32, (own, width), 1)
    line = lax.broadcasted_iota(jnp.int32, (own, width), 0)
    first = start_b + column * width
    total = vir.shape[0]

    def put(s, acc):
        orb = first + s
        value = jnp.where(orb < total, vir_e[jnp.minimum(orb, total - 1)], 0.0)
        return jnp.where(slot == column * width + s, value, acc)

    eps_b = lax.fori_loop(0, width, put, jnp.zeros((own, width), F32))
    eps_ij = jnp.zeros((own, width), F32)
    for p in range(own):
        i, j = pair_list[y * own + p, 0], pair_list[y * own + p, 1]
        eps_ij = jnp.where(line == p, occ_e[i] + occ_e[j], eps_ij)
    denom[...] = eps_ij - vir_e[a_orb] - eps_b
    live[...] = (slot < count_b).astype(jnp.int32)


def labels(place, vir, occ, allowed, pair_list, occ_e, vir_e, width, own, pairs):
    total = vir.shape[0]
    cells = vir.reshape(4, total // 32, 8)
    mine = lax.dynamic_index_in_dim(cells, place[0], 0, keepdims=False)
    return pl.pallas_call(
        labels_body,
        out_shape=(
            jax.ShapeDtypeStruct((total // 32, 8 * pairs), jnp.int32),
            jax.ShapeDtypeStruct((own, width), F32),
            jax.ShapeDtypeStruct((own, width), jnp.int32),
        ),
        in_specs=[smem()] * 7 + [vmem()] * 2,
        out_specs=(vmem(),) * 3,
        cost_estimate=pl.CostEstimate(flops=1000, bytes_accessed=2 * MIB, transcendentals=0),
    )(place, vir, occ, allowed, pair_list, occ_e, vir_e, vir.reshape(8, total // 8), mine)


STEP = 4


def ladder_body(last, base, groups, place, bound, slab, *rest):
    pieces = rest[:16]
    rest = rest[16:]
    if last:
        before, cyc0, cyc1, o0, o1, o2, o3 = rest[:7]
        rest = rest[7:]
    else:
        (out,) = rest[:1]
        rest = rest[1:]
    ints, amps, acc, final, int_sems, amp_sems = rest
    y, x, z, core = place[0], place[1], place[2], place[3]
    steps = groups // STEP

    def int_copy(s):
        return pltpu.make_async_copy(
            slab.at[:, pl.ds((base + s * STEP) * 8, STEP * 8), :], ints.at[s % 2], int_sems.at[s % 2]
        )

    def amp_copies(s, is_core):
        half = (s * STEP) // 8
        inner = (s * STEP) % 8
        out = []
        for side in range(2):
            k = is_core if side == 0 else 1 - is_core
            for g, shift in enumerate((0, 3, 1, 2)):
                source = pieces[(side * 4 + g) * 2 + half].at[pl.ds(inner, STEP)]
                if k == 0:
                    target = amps.at[s % 2, :, :, lax.rem(z + shift, 4), 0]
                else:
                    target = amps.at[s % 2, :, lax.rem(x + shift, 4), :, 1]
                out.append(pltpu.make_async_copy(source, target, amp_sems.at[s % 2, side * 4 + g]))
        return out

    def start(s):
        int_copy(s).start()
        for c in range(2):

            @pl.when(core == c)
            def _(c=c):
                for copy in amp_copies(s, c):
                    copy.start()

    def wait(s):
        int_copy(s).wait()
        for c in range(2):

            @pl.when(core == c)
            def _(c=c):
                for copy in amp_copies(s, c):
                    copy.wait()

    width = slab.shape[0]
    lanes = acc.shape[1]
    slots = slab.shape[2]
    t_of = lax.broadcasted_iota(jnp.int32, (slots, lanes), 0)
    acc[...] = jnp.zeros_like(acc)
    start(0)
    for s in range(steps):
        if s + 1 < steps:
            start(s + 1)
        wait(s)

        def one(g, carry, s=s):
            amp = amps[s % 2, g].reshape(slots, lanes)
            edge = bound[pl.ds(base + s * STEP + g, 1), :]
            high, low = split(jnp.where(t_of < edge, amp, 0.0))
            block = ints[s % 2, :, pl.ds(pl.multiple_of(g * 8, 8), 8), :].reshape(width * 8, slots)
            int_high, int_low = split(block)
            acc[...] += (
                jnp.dot(int_high, high, preferred_element_type=F32)
                + jnp.dot(int_high, low, preferred_element_type=F32)
                + jnp.dot(int_low, high, preferred_element_type=F32)
            )
            return carry

        lax.fori_loop(0, STEP, one, 0)
    pairs = lanes // 8
    shape = (width, 8, lanes)
    same = lax.broadcasted_iota(jnp.int32, shape, 1) == lax.div(lax.broadcasted_iota(jnp.int32, shape, 2), pairs)
    folded = jnp.sum(jnp.where(same, acc[...].reshape(shape), 0.0), axis=1)
    total = folded[:, :pairs]
    for j in range(1, 8):
        total = total + folded[:, j * pairs : (j + 1) * pairs]
    total = total.T
    if not last:
        out[...] = total
        return
    final[...] = total + before[...] + cyc0[...] + cyc1[...]
    own = pairs // 4
    for o, shift in ((o0, 0), (o1, 1), (o2, 3), (o3, 2)):
        o[...] = final[pl.ds(pl.multiple_of(lax.rem(y + shift, 4) * own, 8), own), :]


def ladder(place, bound, slab, pieces, base, extra=None):
    last = extra is not None
    width, cells, slots = slab.shape
    groups = 2 * pieces[0].shape[0]
    lanes = pieces[0].shape[3]
    pairs = lanes // 8
    if last:
        out_shape = (jax.ShapeDtypeStruct((pairs // 4, width), F32),) * 4
        out_specs = (vmem(),) * 4
    else:
        out_shape = jax.ShapeDtypeStruct((pairs, width), F32)
        out_specs = vmem()
        extra = ()
    return pl.pallas_call(
        functools.partial(ladder_body, last, base, groups),
        out_shape=out_shape,
        in_specs=[smem(), vmem(), hbm()] + [hbm()] * 16 + [vmem()] * len(extra),
        out_specs=out_specs,
        scratch_shapes=[
            pltpu.VMEM((2, width, STEP * 8, slots), F32),
            pltpu.VMEM((2, STEP, 4, 4, 2, 8, lanes), F32),
            pltpu.VMEM((width * 8, lanes), F32),
            pltpu.VMEM((pairs, width), F32),
            pltpu.SemaphoreType.DMA((2,)),
            pltpu.SemaphoreType.DMA((2, 8)),
        ],
        compiler_params=pltpu.CompilerParams(vmem_limit_bytes=40 * MIB),
        cost_estimate=pl.CostEstimate(
            flops=2 * 3 * groups * width * 8 * slots * lanes, bytes_accessed=groups * MIB // 2, transcendentals=0
        ),
    )(place, bound, slab, *pieces, *extra)


def on_device(vir, occ, allowed, pair_list, occ_e, vir_e, ladder_amp, int_slab, cycle_amp, cycle_int):
    row, column = lax.axis_index("row"), lax.axis_index("column")
    place = jnp.stack(
        [lax.axis_index("depth"), row // 2, (row % 2) * 2 + column // 2, column % 2]
    ).astype(jnp.int32)
    pairs = ladder_amp.shape[0]
    width = int_slab.shape[1]
    own = pairs // 4

    mine = relayout(jnp.transpose(ladder_amp, (0, 2, 1)))
    blocks = [mine] + [send(mine, FIRST[n]) for n in (1, -1, 2)]
    quarters = stack(place, blocks)
    below = [send(q, SECOND[1]) for q in quarters]
    above = [send(q, SECOND[-1]) for q in quarters]
    across = [send(below[i], SECOND[1]) if i % 2 == 0 else send(above[i], SECOND[-1]) for i in range(4)]

    bound, denom, live = labels(place, vir, occ, allowed, pair_list, occ_e, vir_e, width, own, pairs)
    choice = (pair_list[:, 1:] == jnp.arange(cycle_int.shape[1], dtype=jnp.int32)).astype(F32)
    choice = jnp.repeat(choice, cycle_amp.shape[1], axis=0)
    c0, c1, c2, c3 = cycle(place, cycle_amp, jnp.transpose(cycle_int, (1, 2, 0)), choice)
    keep, away = join(place, (c0, send(c1, ALONG_X[1]), send(c2, ALONG_X[-1]), send(c3, ALONG_X[2])))
    got = send(away, Z_ACROSS)

    slab = int_slab.reshape(int_slab.shape[1:])
    held = []
    for i in range(4):
        held.append([quarters[i], below[i], above[i], across[i]])
    other = [[send(v, SWAP) for v in h] for h in held]
    sums = None
    for half in range(2):
        pieces = []
        for side in (held, other):
            for g in range(4):
                pieces += [side[2 * half][g], side[2 * half + 1][g]]
        extra = (sums, keep, got) if half else None
        sums = ladder(place, bound, slab, pieces, half * 16, extra)
    s0, s1, s2, s3 = sums
    total = s0 + send(s1, ALONG_Y[1]) + send(s2, ALONG_Y[-1]) + send(s3, ALONG_Y[2])
    return jnp.where(live > 0, total / denom, jnp.float32(0.0))[None]


def solution(mesh):
    return jax.shard_map(
        on_device,
        mesh=mesh,
        in_specs=(
            P(),
            P(),
            P(),
            P(),
            P(),
            P(),
            P(None, "depth", ("row", "column")),
            P("row", "column", "depth", None),
            P(None, None, ("depth", "row")),
            P(("depth", "row"), None, "column"),
        ),
        out_specs=P("row", "depth", "column"),
        check_vma=False,
    )
```

```python
import functools

import jax
import jax.numpy as jnp
from jax import lax
from jax.experimental import pallas as pl
from jax.experimental.pallas import tpu as pltpu
from jax.sharding import PartitionSpec as P

AXES = ("depth", "row", "column")
F32 = jnp.float32
BF16 = jnp.bfloat16
MIB = 1 << 20


def pairs_of(core0, core1):
    out = []
    for y in range(4):
        for x in range(4):
            for z in range(4):
                for k in range(2):
                    ty, tx, tz, tk = (core1 if k else core0)(y, x, z, k)
                    out.append((y * 32 + x * 8 + z * 2 + k, (ty % 4) * 32 + (tx % 4) * 8 + (tz % 4) * 2 + tk % 2))
    return out


def along_x(n):
    return lambda y, x, z, k: (y, x + n, z, k)


def along_y(n):
    return lambda y, x, z, k: (y + n, x, z, k)


def along_z(n):
    return lambda y, x, z, k: (y, x, z + n, k)


def other_core(y, x, z, k):
    return (y, x, z, k + 1)


FIRST = {n: pairs_of(along_x(n), along_z(n)) for n in (1, -1, 2)}
SECOND = {n: pairs_of(along_z(n), along_x(n)) for n in (1, -1, 2)}
ALONG_X = {n: pairs_of(along_x(n), along_x(n)) for n in (1, -1, 2)}
ALONG_Y = {n: pairs_of(along_y(n), along_y(n)) for n in (1, -1, 2)}
Z_ACROSS = pairs_of(along_z(2), along_z(2))
SWAP = pairs_of(other_core, other_core)


def send(value, pairs):
    return lax.ppermute(value, AXES, pairs)


def spread(parts, line):
    return (parts[0], send(parts[1], line[1]), send(parts[2], line[-1]), send(parts[3], line[2]))


def smem():
    return pl.BlockSpec(memory_space=pltpu.SMEM)


def vmem():
    return pl.BlockSpec(memory_space=pltpu.VMEM)


def anywhere():
    return pl.BlockSpec(memory_space=pl.ANY)


def in_vmem(value):
    return pltpu.with_memory_space_constraint(value, pltpu.VMEM)


def in_hbm(value):
    return pltpu.with_memory_space_constraint(value, pltpu.HBM)


def grant(mib):
    return pltpu.CompilerParams(vmem_limit_bytes=mib * MIB)


def small_cost():
    return pl.CostEstimate(flops=1, bytes_accessed=1, transcendentals=0)


CELLS = 4


def relayout_body(amp_ref, out_ref, turned):
    pairs, slots, cells = amp_ref.shape
    groups = cells // CELLS
    for t in range(slots):
        turned[t] = amp_ref[:, t, :].T
    for t in range(slots):
        pieces = [turned[t, pl.ds(j, groups, stride=CELLS), :] for j in range(CELLS)]
        out_ref[:, t, :] = jnp.concatenate(pieces, axis=1)


def relayout(amp):
    pairs, slots, cells = amp.shape
    return pl.pallas_call(
        relayout_body,
        out_shape=jax.ShapeDtypeStruct((cells // CELLS, slots, CELLS * pairs), F32),
        in_specs=[vmem()],
        out_specs=vmem(),
        scratch_shapes=[pltpu.VMEM((slots, cells, pairs), F32)],
        compiler_params=grant(8),
        cost_estimate=small_cost(),
    )(amp)


def stack_body(place, b0, b1, b2, b3, after, out):
    own = jnp.where(place[3] == 0, place[1], place[2])
    for source, shift in ((b0, 0), (b1, 3), (b2, 1), (b3, 2)):
        out[:, pl.ds(lax.rem(own + shift, 4), 1)] = source[...][:, None]


def stack(place, blocks, after):
    groups, slots, lanes = blocks[0].shape
    return pl.pallas_call(
        stack_body,
        out_shape=jax.ShapeDtypeStruct((groups, 4, slots, lanes), F32),
        in_specs=[smem()] + [vmem()] * 4 + [anywhere()],
        out_specs=vmem(),
        compiler_params=grant(8),
        cost_estimate=small_cost(),
    )(place, *blocks, after)


CHUNKS = (32, 32)


def pack_body(base, place, p0, p1, p2, p3, *rest):
    out = rest[-1]
    count = out.shape[0]
    x, z, core = place[1], place[2], place[3]
    for piece, shift in ((p0, 0), (p1, 3), (p2, 1), (p3, 2)):
        first = jnp.where(core == 0, lax.rem(z + shift, 4), lax.rem(x + shift, 4) * 4)
        for i in range(4):
            out[:, pl.ds(first + i * jnp.where(core == 0, 4, 1), 1)] = piece[base : base + count, i : i + 1]


def pack(place, pieces, base, count, after):
    _, _, slots, lanes = pieces[0].shape
    return pl.pallas_call(
        functools.partial(pack_body, base),
        out_shape=jax.ShapeDtypeStruct((count, 16, slots, lanes), F32),
        in_specs=[smem()] + [vmem()] * 4 + [anywhere()] * len(after),
        out_specs=vmem(),
        compiler_params=grant(12),
        cost_estimate=small_cost(),
    )(place, *pieces, *after)


def dot_nt(a, b):
    return lax.dot_general(a, b, (((1,), (1,)), ((), ())), preferred_element_type=F32)


def split(value):
    high = value.astype(BF16)
    return high, (value - high.astype(F32)).astype(BF16)


DEPTH_BLOCK = 1280


def cycle_body(depth, place, amp_ref, int_ref, choice_ref, after, o0, o1, o2, o3, acc, by_row):
    step = pl.program_id(0)
    window, width, block = int_ref.shape
    pairs, rows, _ = amp_ref.shape

    @pl.when(step == 0)
    def _():
        acc[...] = jnp.zeros_like(acc)

    left = depth - step * block
    amp = amp_ref[...].reshape(pairs * rows, block)
    ints = int_ref[...].reshape(window * width, block)
    inside = lax.broadcasted_iota(jnp.int32, amp.shape, 1) < left
    high, low = split(jnp.where(inside, amp, 0.0))
    inside = lax.broadcasted_iota(jnp.int32, ints.shape, 1) < left
    int_high, int_low = split(jnp.where(inside, ints, 0.0))
    acc[...] += dot_nt(high, int_high) + dot_nt(high, int_low) + dot_nt(low, int_high)

    @pl.when(step == pl.num_programs(0) - 1)
    def _():
        total = jnp.zeros((pairs * rows, width), F32)
        for j in range(window):
            total = total + choice_ref[:, j : j + 1] * acc[:, j * width : (j + 1) * width]
        by_row[...] = total
        own = pairs // 4
        for out, shift in ((o0, 0), (o1, 1), (o2, 3), (o3, 2)):
            at = lax.rem(place[0] + shift, 4) * own * rows
            for a in range(rows):
                out[a] = by_row[pl.ds(at + a, own, stride=rows), :]


def cycle(place, amp, ints, choice, after):
    pairs, rows, depth = amp.shape
    window, width, _ = ints.shape
    part = jax.ShapeDtypeStruct((rows, pairs // 4, width), F32)
    whole = pl.BlockSpec(part.shape, lambda i: (0, 0, 0))
    return pl.pallas_call(
        functools.partial(cycle_body, depth),
        grid=(pl.cdiv(depth, DEPTH_BLOCK),),
        out_shape=(part,) * 4,
        in_specs=[
            smem(),
            pl.BlockSpec((pairs, rows, DEPTH_BLOCK), lambda i: (0, 0, i)),
            pl.BlockSpec((window, width, DEPTH_BLOCK), lambda i: (0, 0, i)),
            pl.BlockSpec((pairs * rows, window), lambda i: (0, 0)),
            anywhere(),
        ],
        out_specs=(whole,) * 4,
        scratch_shapes=[
            pltpu.VMEM((pairs * rows, window * width), F32),
            pltpu.VMEM((pairs * rows, width), F32),
        ],
        compiler_params=grant(24),
        cost_estimate=small_cost(),
    )(place, in_hbm(amp), in_hbm(ints), choice, after)


def rows_body(place, a0, a1, a2, a3, *rest):
    o0, o1, o2, o3, held = rest[-5:]
    held[...] = a0[...] + a1[...] + a2[...] + a3[...]
    for out, shift in ((o0, 0), (o1, 1), (o2, 3), (o3, 2)):
        out[...] = held[pl.ds(lax.rem(place[1] + shift, 4) * 2, 2)]


def rows(place, parts, after):
    count, own, width = parts[0].shape
    return pl.pallas_call(
        rows_body,
        out_shape=(jax.ShapeDtypeStruct((count // 4, own, width), F32),) * 4,
        in_specs=[smem()] + [vmem()] * 4 + [anywhere()] * len(after),
        out_specs=(vmem(),) * 4,
        scratch_shapes=[pltpu.VMEM((count, own, width), F32)],
        compiler_params=grant(8),
        cost_estimate=small_cost(),
    )(place, *parts, *after)


def halves_body(place, a0, a1, a2, a3, *rest):
    keep, away = rest[-2:]
    half = lax.div(place[2], 2)
    total = a0[...] + a1[...] + a2[...] + a3[...]
    keep[...] = jnp.where(half == 0, total[0], total[1])
    away[...] = jnp.where(half == 0, total[1], total[0])


def halves(place, parts, after):
    one = jax.ShapeDtypeStruct(parts[0].shape[1:], F32)
    return pl.pallas_call(
        halves_body,
        out_shape=(one, one),
        in_specs=[smem()] + [vmem()] * 4 + [anywhere()] * len(after),
        out_specs=(vmem(), vmem()),
        compiler_params=grant(8),
        cost_estimate=small_cost(),
    )(place, *parts, *after)


def labels_body(place, vir, occ, allowed, pair_list, occ_e, vir_e, vir_tile, bound, denom, live):
    y, x, z, core = place[0], place[1], place[2], place[3]
    row = x * 2 + lax.div(z, 2)
    column = lax.rem(z, 2) * 2 + core
    irreps = allowed.shape[0]
    total = vir.shape[0]
    pair_irrep = jnp.bitwise_xor(occ[pair_list[0, 0]], occ[pair_list[1, 0]])
    a_orb = row * 128
    ga = vir[a_orb]
    gb = jnp.bitwise_xor(ga, pair_irrep)
    tile = vir_tile[...]
    counts = [jnp.sum((tile == g).astype(jnp.int32)) for g in range(irreps)]
    starts = [jnp.int32(0)]
    for g in range(irreps - 1):
        starts.append(starts[g] + counts[g])
    count_b = jnp.int32(0)
    start_b = jnp.int32(0)
    groups, lanes = bound.shape
    cell = (
        y * (groups * CELLS)
        + lax.broadcasted_iota(jnp.int32, bound.shape, 0) * CELLS
        + lax.div(lax.broadcasted_iota(jnp.int32, bound.shape, 1), lanes // CELLS)
    )
    limit = jnp.zeros(bound.shape, jnp.int32)
    for g in range(irreps):
        count_b = jnp.where(gb == g, counts[g], count_b)
        start_b = jnp.where(gb == g, starts[g], start_b)
        partner = jnp.bitwise_xor(pair_irrep, g)
        reach = jnp.int32(0)
        for h in range(irreps):
            reach = jnp.where(partner == h, counts[h], reach)
        reach = reach * allowed[ga, gb, g]
        limit = jnp.where((cell >= starts[g]) & (cell < starts[g] + counts[g]), reach, limit)
    bound[...] = limit
    own, width = denom.shape
    slot = column * width + lax.broadcasted_iota(jnp.int32, (own, width), 1)
    line = lax.broadcasted_iota(jnp.int32, (own, width), 0)
    first = start_b + column * width

    def put(s, acc):
        orb = first + s
        value = jnp.where(orb < total, vir_e[jnp.minimum(orb, total - 1)], 0.0)
        return jnp.where(slot == column * width + s, value, acc)

    eps_b = lax.fori_loop(0, width, put, jnp.zeros((own, width), F32))
    eps_ij = jnp.zeros((own, width), F32)
    for p in range(own):
        i, j = pair_list[0, y * own + p], pair_list[1, y * own + p]
        eps_ij = jnp.where(line == p, occ_e[i] + occ_e[j], eps_ij)
    denom[...] = eps_ij - vir_e[a_orb] - eps_b
    live[...] = (slot < count_b).astype(jnp.int32)


def labels(place, vir, occ, allowed, pair_list, occ_e, vir_e, width, own, pairs):
    total = vir.shape[0]
    return pl.pallas_call(
        labels_body,
        out_shape=(
            jax.ShapeDtypeStruct((total // 4 // CELLS, CELLS * pairs), jnp.int32),
            jax.ShapeDtypeStruct((own, width), F32),
            jax.ShapeDtypeStruct((own, width), jnp.int32),
        ),
        in_specs=[smem()] * 7 + [vmem()],
        out_specs=(vmem(),) * 3,
        compiler_params=grant(8),
        cost_estimate=small_cost(),
    )(place, vir, occ, allowed, pair_list.T, occ_e, vir_e, vir.reshape(8, total // 8))


READY = 4
SLOTS = 3
PARTS = 4


def ready_body(slab, after, out, token, held, sems):
    token[...] = jnp.zeros_like(token)
    width, cells, slots = slab.shape
    steps = cells // (8 * READY)
    share = width // PARTS

    def copies(s):
        return [
            pltpu.make_async_copy(
                slab.at[pl.ds(n * share, share), pl.ds(s * READY * 8, READY * 8), :],
                held.at[s % SLOTS, pl.ds(n * share, share)],
                sems.at[s % SLOTS, n],
            )
            for n in range(PARTS)
        ]

    for s in range(SLOTS - 1):
        for c in copies(s):
            c.start()
    for s in range(steps):
        if s + SLOTS - 1 < steps:
            for c in copies(s + SLOTS - 1):
                c.start()
        for c in copies(s):
            c.wait()
        for g in range(READY):
            block = held[s % SLOTS, :, 8 * g : 8 * g + 8, :].reshape(width // 2, 2, 8, slots)
            even, odd = block[:, 0], block[:, 1]
            first = lax.broadcasted_iota(jnp.int32, even.shape, 1) < CELLS
            lower_cells = jnp.where(first, even, pltpu.roll(odd, CELLS, 1)).reshape(width * CELLS, slots)
            upper_cells = jnp.where(first, pltpu.roll(even, CELLS, 1), odd).reshape(width * CELLS, slots)
            for i, rows in enumerate((lower_cells, upper_cells)):
                at = (s * READY + g) * 2 + i
                high, low = split(rows)
                out[at, pl.ds(0, width * CELLS)] = high
                out[at, pl.ds(width * CELLS, width * CELLS)] = low


def ready(slab, after):
    width, cells, slots = slab.shape
    return pl.pallas_call(
        ready_body,
        out_shape=(
            jax.ShapeDtypeStruct((cells // CELLS, 2 * CELLS * width, slots), BF16),
            jax.ShapeDtypeStruct((8, 128), F32),
        ),
        in_specs=[anywhere(), anywhere()],
        out_specs=(vmem(), vmem()),
        scratch_shapes=[
            pltpu.VMEM((SLOTS, width, READY * 8, slots), F32),
            pltpu.SemaphoreType.DMA((SLOTS, PARTS)),
        ],
        compiler_params=grant(28),
        cost_estimate=small_cost(),
    )(slab, after)


STEP = 8


def ladder_body(last, base, place, bound, slab, mine, other, before, after, *rest):
    if last:
        o0, o1, o2, o3, amps, acc, folded, final = rest
    else:
        out, amps, acc, folded, final = rest
    y, core = place[0], place[3]
    _, rows, slots = slab.shape
    lanes = bound.shape[1]
    width = rows // (2 * CELLS)
    pairs = lanes // CELLS
    t_of = lax.broadcasted_iota(jnp.int32, (slots, lanes), 0)
    for s in range(mine.shape[0] // STEP):
        left, right = [], []
        for g in range(STEP):
            amps[g, :, pl.ds(core, 1)] = mine[s * STEP + g][:, None]
            amps[g, :, pl.ds(1 - core, 1)] = other[s * STEP + g][:, None]
            at = base + s * STEP + g
            edge = bound[at : at + 1, :]
            high, low = split(jnp.where(t_of < edge, amps[g].reshape(slots, lanes), 0.0))
            left.append(slab[at])
            right.append(jnp.concatenate([high, low], axis=1))
        part = jnp.dot(jnp.concatenate(left, axis=1), jnp.concatenate(right, axis=0), preferred_element_type=F32)
        if s == 0:
            acc[...] = part
        else:
            acc[...] += part
    half = rows // 2
    folded[...] = (acc[:half, :lanes] + acc[:half, lanes:]) + (acc[half:, :lanes] + acc[half:, lanes:])
    total = jnp.zeros((width, pairs), F32)
    for j in range(CELLS):
        total = total + folded[pl.ds(j, width, stride=CELLS), :][:, j * pairs : (j + 1) * pairs]
    total = total.T
    if not last:
        out[...] = total if base == 0 else total + before[...]
        return
    if base:
        total = total + before[...]
    final[...] = total
    own = pairs // 4
    for o, shift in ((o0, 0), (o1, 1), (o2, 3), (o3, 2)):
        o[...] = final[pl.ds(pl.multiple_of(lax.rem(y + shift, 4) * own, 8), own), :]


def ladder(place, bound, slab, mine, other, base, before, after, last):
    _, rows, slots = slab.shape
    lanes = bound.shape[1]
    pairs = lanes // CELLS
    width = rows // (2 * CELLS)
    if last:
        out_shape = (jax.ShapeDtypeStruct((pairs // 4, width), F32),) * 4
        out_specs = (vmem(),) * 4
    else:
        out_shape = jax.ShapeDtypeStruct((pairs, width), F32)
        out_specs = vmem()
    return pl.pallas_call(
        functools.partial(ladder_body, last, base),
        out_shape=out_shape,
        in_specs=[smem()] + [vmem()] * 5 + [anywhere()],
        out_specs=out_specs,
        scratch_shapes=[
            pltpu.VMEM((STEP, slots // 16, 2, 8, lanes), F32),
            pltpu.VMEM((rows, 2 * lanes), F32),
            pltpu.VMEM((rows // 2, lanes), F32),
            pltpu.VMEM((pairs, width), F32),
        ],
        compiler_params=grant(12),
        cost_estimate=small_cost(),
    )(place, bound, in_vmem(slab), mine, other, before, after)


def on_device(vir, occ, allowed, pair_list, occ_e, vir_e, ladder_amp, int_slab, cycle_amp, cycle_int):
    row, column = lax.axis_index("row"), lax.axis_index("column")
    place = jnp.stack(
        [lax.axis_index("depth"), row // 2, (row % 2) * 2 + column // 2, column % 2]
    ).astype(jnp.int32)
    pairs = ladder_amp.shape[0]
    width = int_slab.shape[1]
    own = pairs // 4

    mine = relayout(jnp.transpose(ladder_amp, (0, 2, 1)))
    bound, denom, live = labels(place, vir, occ, allowed, pair_list, occ_e, vir_e, width, own, pairs)
    line = stack(place, [mine] + [send(mine, FIRST[n]) for n in (1, -1, 2)], bound)
    pieces = [line] + [send(line, SECOND[n]) for n in (1, -1, 2)]

    choice = (pair_list[:, 1:] == jnp.arange(cycle_int.shape[1], dtype=jnp.int32)).astype(F32)
    choice = jnp.repeat(choice, cycle_amp.shape[1], axis=0)
    parts = cycle(place, cycle_amp, jnp.transpose(cycle_int, (1, 2, 0)), choice, line)
    slab, token = ready(in_hbm(int_slab.reshape(int_slab.shape[1:])), parts[0])

    parts = rows(place, spread(parts, ALONG_Y), (token,))
    base, sums, last_packed, keep = 0, bound, parts[0], parts[0]
    for i, count in enumerate(CHUNKS):
        packed = pack(place, pieces, base, count, (last_packed,))
        other = send(packed, SWAP)
        if i == 0:
            parts = spread(parts, ALONG_X)
        sums = ladder(place, bound, slab, packed, other, base, sums, keep, i == len(CHUNKS) - 1)
        if i == 0:
            keep, away = halves(place, parts, (sums,))
            got = send(away, Z_ACROSS)
        base += count
        last_packed = packed
    s0, s1, s2, s3 = spread(sums, ALONG_Y)
    total = (s0 + s1) + (s2 + s3) + (keep + got)
    return jnp.where(live > 0, total / denom, jnp.float32(0.0))[None]


def solution(mesh):
    return jax.shard_map(
        on_device,
        mesh=mesh,
        in_specs=(
            P(),
            P(),
            P(),
            P(),
            P(),
            P(),
            P(None, "depth", ("row", "column")),
            P("row", "column", "depth", None),
            P(None, None, ("depth", "row")),
            P(("depth", "row"), None, "column"),
        ),
        out_specs=P("row", "depth", "column"),
        check_vma=False,
    )
```

```python
import functools

import jax
import jax.numpy as jnp
from jax import lax
from jax.experimental import pallas as pl
from jax.experimental.pallas import tpu as pltpu
from jax.sharding import PartitionSpec as P

AXES = ("depth", "row", "column")
F32 = jnp.float32
BF16 = jnp.bfloat16
MIB = 1 << 20


def pairs_of(core0, core1):
    out = []
    for y in range(4):
        for x in range(4):
            for z in range(4):
                for k in range(2):
                    ty, tx, tz, tk = (core1 if k else core0)(y, x, z, k)
                    out.append((y * 32 + x * 8 + z * 2 + k, (ty % 4) * 32 + (tx % 4) * 8 + (tz % 4) * 2 + tk % 2))
    return out


def along_x(n):
    return lambda y, x, z, k: (y, x + n, z, k)


def along_y(n):
    return lambda y, x, z, k: (y + n, x, z, k)


def along_z(n):
    return lambda y, x, z, k: (y, x, z + n, k)


def other_core(y, x, z, k):
    return (y, x, z, k + 1)


FIRST = {n: pairs_of(along_x(n), along_z(n)) for n in (1, -1, 2)}
SECOND = {n: pairs_of(along_z(n), along_x(n)) for n in (1, -1, 2)}
ALONG_X = {n: pairs_of(along_x(n), along_x(n)) for n in (1, -1, 2)}
ALONG_Y = {n: pairs_of(along_y(n), along_y(n)) for n in (1, -1, 2)}
Z_ACROSS = pairs_of(along_z(2), along_z(2))
SWAP = pairs_of(other_core, other_core)


def send(value, pairs):
    return lax.ppermute(value, AXES, pairs)


def spread(parts, line):
    return (parts[0], send(parts[1], line[1]), send(parts[2], line[-1]), send(parts[3], line[2]))


def smem():
    return pl.BlockSpec(memory_space=pltpu.SMEM)


def vmem():
    return pl.BlockSpec(memory_space=pltpu.VMEM)


def anywhere():
    return pl.BlockSpec(memory_space=pl.ANY)


def in_vmem(value):
    return pltpu.with_memory_space_constraint(value, pltpu.VMEM)


def in_hbm(value):
    return pltpu.with_memory_space_constraint(value, pltpu.HBM)


def grant(mib):
    return pltpu.CompilerParams(vmem_limit_bytes=mib * MIB)


def small_cost():
    return pl.CostEstimate(flops=1, bytes_accessed=1, transcendentals=0)


CELLS = 4


def relayout_body(amp_ref, out_ref, turned):
    pairs, slots, cells = amp_ref.shape
    groups = cells // CELLS
    for t in range(slots):
        turned[t] = amp_ref[:, t, :].T
    for t in range(slots):
        pieces = [turned[t, pl.ds(j, groups, stride=CELLS), :] for j in range(CELLS)]
        out_ref[:, t, :] = jnp.concatenate(pieces, axis=1)


def relayout(amp):
    pairs, slots, cells = amp.shape
    return pl.pallas_call(
        relayout_body,
        out_shape=jax.ShapeDtypeStruct((cells // CELLS, slots, CELLS * pairs), F32),
        in_specs=[vmem()],
        out_specs=vmem(),
        scratch_shapes=[pltpu.VMEM((slots, cells, pairs), F32)],
        compiler_params=grant(8),
        cost_estimate=small_cost(),
    )(amp)


def stack_body(place, b0, b1, b2, b3, after, out):
    own = jnp.where(place[3] == 0, place[1], place[2])
    for source, shift in ((b0, 0), (b1, 3), (b2, 1), (b3, 2)):
        out[:, pl.ds(lax.rem(own + shift, 4), 1)] = source[...][:, None]


def stack(place, blocks, after):
    groups, slots, lanes = blocks[0].shape
    return pl.pallas_call(
        stack_body,
        out_shape=jax.ShapeDtypeStruct((groups, 4, slots, lanes), F32),
        in_specs=[smem()] + [vmem()] * 4 + [anywhere()],
        out_specs=vmem(),
        compiler_params=grant(8),
        cost_estimate=small_cost(),
    )(place, *blocks, after)


CHUNKS = (32, 32)


def pack_body(place, p0, p1, p2, p3, *rest):
    out = rest[-len(CHUNKS) :]
    x, z, core = place[1], place[2], place[3]
    base = 0
    for o in out:
        count = o.shape[0]
        for piece, shift in ((p0, 0), (p1, 3), (p2, 1), (p3, 2)):
            first = jnp.where(core == 0, lax.rem(z + shift, 4), lax.rem(x + shift, 4) * 4)
            for i in range(4):
                o[:, pl.ds(first + i * jnp.where(core == 0, 4, 1), 1)] = piece[base : base + count, i : i + 1]
        base += count


def pack(place, pieces, after):
    _, _, slots, lanes = pieces[0].shape
    return pl.pallas_call(
        pack_body,
        out_shape=tuple(jax.ShapeDtypeStruct((n, 16, slots, lanes), F32) for n in CHUNKS),
        in_specs=[smem()] + [vmem()] * 4 + [anywhere()] * len(after),
        out_specs=(vmem(),) * len(CHUNKS),
        compiler_params=grant(12),
        cost_estimate=small_cost(),
    )(place, *pieces, *after)


def dot_nt(a, b):
    return lax.dot_general(a, b, (((1,), (1,)), ((), ())), preferred_element_type=F32)


def split(value):
    high = value.astype(BF16)
    return high, (value - high.astype(F32)).astype(BF16)


DEPTH_BLOCK = 1280


def cycle_body(depth, place, amp_ref, int_ref, choice_ref, o0, o1, o2, o3, acc, by_row):
    step = pl.program_id(0)
    window, width, block = int_ref.shape
    pairs, rows, _ = amp_ref.shape

    @pl.when(step == 0)
    def _():
        acc[...] = jnp.zeros_like(acc)

    left = depth - step * block
    amp = amp_ref[...].reshape(pairs * rows, block)
    ints = int_ref[...].reshape(window * width, block)
    inside = lax.broadcasted_iota(jnp.int32, amp.shape, 1) < left
    high, low = split(jnp.where(inside, amp, 0.0))
    inside = lax.broadcasted_iota(jnp.int32, ints.shape, 1) < left
    int_high, int_low = split(jnp.where(inside, ints, 0.0))
    acc[...] += dot_nt(high, int_high) + dot_nt(high, int_low) + dot_nt(low, int_high)

    @pl.when(step == pl.num_programs(0) - 1)
    def _():
        total = jnp.zeros((pairs * rows, width), F32)
        for j in range(window):
            total = total + choice_ref[:, j : j + 1] * acc[:, j * width : (j + 1) * width]
        by_row[...] = total
        own = pairs // 4
        for out, shift in ((o0, 0), (o1, 1), (o2, 3), (o3, 2)):
            at = lax.rem(place[0] + shift, 4) * own * rows
            for a in range(rows):
                out[a] = by_row[pl.ds(at + a, own, stride=rows), :]


def cycle(place, amp, ints, choice):
    pairs, rows, depth = amp.shape
    window, width, _ = ints.shape
    part = jax.ShapeDtypeStruct((rows, pairs // 4, width), F32)
    whole = pl.BlockSpec(part.shape, lambda i: (0, 0, 0))
    return pl.pallas_call(
        functools.partial(cycle_body, depth),
        grid=(pl.cdiv(depth, DEPTH_BLOCK),),
        out_shape=(part,) * 4,
        in_specs=[
            smem(),
            pl.BlockSpec((pairs, rows, DEPTH_BLOCK), lambda i: (0, 0, i)),
            pl.BlockSpec((window, width, DEPTH_BLOCK), lambda i: (0, 0, i)),
            pl.BlockSpec((pairs * rows, window), lambda i: (0, 0)),
        ],
        out_specs=(whole,) * 4,
        scratch_shapes=[
            pltpu.VMEM((pairs * rows, window * width), F32),
            pltpu.VMEM((pairs * rows, width), F32),
        ],
        compiler_params=grant(24),
        cost_estimate=small_cost(),
    )(place, in_hbm(amp), in_hbm(ints), choice)


def by_half_body(place, a0, a1, a2, a3, after, keep, away, held):
    held[...] = a0[...] + a1[...] + a2[...] + a3[...]
    half = lax.div(place[2], 2)
    for x in range(4):
        keep[pl.ds(x, 1)] = held[pl.ds(2 * x + half, 1)]
        away[pl.ds(x, 1)] = held[pl.ds(2 * x + 1 - half, 1)]


def by_half(place, parts, after):
    count, own, width = parts[0].shape
    return pl.pallas_call(
        by_half_body,
        out_shape=(jax.ShapeDtypeStruct((count // 2, own, width), F32),) * 2,
        in_specs=[smem()] + [vmem()] * 4 + [anywhere()],
        out_specs=(vmem(),) * 2,
        scratch_shapes=[pltpu.VMEM((count, own, width), F32)],
        compiler_params=grant(8),
        cost_estimate=small_cost(),
    )(place, *parts, after)


def by_row_body(place, keep, got, after, o0, o1, o2, o3, held):
    held[...] = keep[...] + got[...]
    for out, shift in ((o0, 0), (o1, 1), (o2, 3), (o3, 2)):
        out[...] = held[lax.rem(place[1] + shift, 4)]


def by_row(place, keep, got, after):
    count, own, width = keep.shape
    return pl.pallas_call(
        by_row_body,
        out_shape=(jax.ShapeDtypeStruct((own, width), F32),) * 4,
        in_specs=[smem()] + [vmem()] * 2 + [anywhere()],
        out_specs=(vmem(),) * 4,
        scratch_shapes=[pltpu.VMEM((count, own, width), F32)],
        compiler_params=grant(8),
        cost_estimate=small_cost(),
    )(place, keep, got, after)


def labels_body(place, vir, occ, allowed, pair_list, occ_e, vir_e, vir_tile, after, bound, denom, live):
    y, x, z, core = place[0], place[1], place[2], place[3]
    row = x * 2 + lax.div(z, 2)
    column = lax.rem(z, 2) * 2 + core
    irreps = allowed.shape[0]
    total = vir.shape[0]
    pair_irrep = jnp.bitwise_xor(occ[pair_list[0, 0]], occ[pair_list[1, 0]])
    a_orb = row * 128
    ga = vir[a_orb]
    gb = jnp.bitwise_xor(ga, pair_irrep)
    tile = vir_tile[...]
    counts = [jnp.sum((tile == g).astype(jnp.int32)) for g in range(irreps)]
    starts = [jnp.int32(0)]
    for g in range(irreps - 1):
        starts.append(starts[g] + counts[g])
    count_b = jnp.int32(0)
    start_b = jnp.int32(0)
    groups, lanes = bound.shape
    cell = (
        y * (groups * CELLS)
        + lax.broadcasted_iota(jnp.int32, bound.shape, 0) * CELLS
        + lax.div(lax.broadcasted_iota(jnp.int32, bound.shape, 1), lanes // CELLS)
    )
    limit = jnp.zeros(bound.shape, jnp.int32)
    for g in range(irreps):
        count_b = jnp.where(gb == g, counts[g], count_b)
        start_b = jnp.where(gb == g, starts[g], start_b)
        partner = jnp.bitwise_xor(pair_irrep, g)
        reach = jnp.int32(0)
        for h in range(irreps):
            reach = jnp.where(partner == h, counts[h], reach)
        reach = reach * allowed[ga, gb, g]
        limit = jnp.where((cell >= starts[g]) & (cell < starts[g] + counts[g]), reach, limit)
    bound[...] = limit
    own, width = denom.shape
    slot = column * width + lax.broadcasted_iota(jnp.int32, (own, width), 1)
    line = lax.broadcasted_iota(jnp.int32, (own, width), 0)
    first = start_b + column * width

    def put(s, acc):
        orb = first + s
        value = jnp.where(orb < total, vir_e[jnp.minimum(orb, total - 1)], 0.0)
        return jnp.where(slot == column * width + s, value, acc)

    eps_b = lax.fori_loop(0, width, put, jnp.zeros((own, width), F32))
    eps_ij = jnp.zeros((own, width), F32)
    for p in range(own):
        i, j = pair_list[0, y * own + p], pair_list[1, y * own + p]
        eps_ij = jnp.where(line == p, occ_e[i] + occ_e[j], eps_ij)
    denom[...] = eps_ij - vir_e[a_orb] - eps_b
    live[...] = (slot < count_b).astype(jnp.int32)


def labels(place, vir, occ, allowed, pair_list, occ_e, vir_e, width, own, pairs, after):
    total = vir.shape[0]
    return pl.pallas_call(
        labels_body,
        out_shape=(
            jax.ShapeDtypeStruct((total // 4 // CELLS, CELLS * pairs), jnp.int32),
            jax.ShapeDtypeStruct((own, width), F32),
            jax.ShapeDtypeStruct((own, width), jnp.int32),
        ),
        in_specs=[smem()] * 7 + [vmem(), anywhere()],
        out_specs=(vmem(),) * 3,
        compiler_params=grant(8),
        cost_estimate=small_cost(),
    )(place, *(in_hbm(v) for v in (vir, occ, allowed, pair_list.T, occ_e, vir_e)), vir.reshape(8, total // 8), after)


READY = 4
SLOTS = 3
PARTS = 4


def ready_body(slab, after, out, token, held, sems):
    token[...] = jnp.zeros_like(token)
    width, cells, slots = slab.shape
    steps = cells // (8 * READY)
    share = width // PARTS

    def copies(s):
        return [
            pltpu.make_async_copy(
                slab.at[pl.ds(n * share, share), pl.ds(s * READY * 8, READY * 8), :],
                held.at[s % SLOTS, pl.ds(n * share, share)],
                sems.at[s % SLOTS, n],
            )
            for n in range(PARTS)
        ]

    for s in range(SLOTS - 1):
        for c in copies(s):
            c.start()
    for s in range(steps):
        if s + SLOTS - 1 < steps:
            for c in copies(s + SLOTS - 1):
                c.start()
        for c in copies(s):
            c.wait()
        for g in range(READY):
            block = held[s % SLOTS, :, 8 * g : 8 * g + 8, :].reshape(width // 2, 2, 8, slots)
            even, odd = block[:, 0], block[:, 1]
            first = lax.broadcasted_iota(jnp.int32, even.shape, 1) < CELLS
            lower_cells = jnp.where(first, even, pltpu.roll(odd, CELLS, 1)).reshape(width * CELLS, slots)
            upper_cells = jnp.where(first, pltpu.roll(even, CELLS, 1), odd).reshape(width * CELLS, slots)
            for i, rows in enumerate((lower_cells, upper_cells)):
                at = (s * READY + g) * 2 + i
                high, low = split(rows)
                out[at, pl.ds(0, width * CELLS)] = high
                out[at, pl.ds(width * CELLS, width * CELLS)] = low


def ready(slab, after):
    width, cells, slots = slab.shape
    return pl.pallas_call(
        ready_body,
        out_shape=(
            jax.ShapeDtypeStruct((cells // CELLS, 2 * CELLS * width, slots), BF16),
            jax.ShapeDtypeStruct((8, 128), F32),
        ),
        in_specs=[anywhere(), anywhere()],
        out_specs=(vmem(), vmem()),
        scratch_shapes=[
            pltpu.VMEM((SLOTS, width, READY * 8, slots), F32),
            pltpu.SemaphoreType.DMA((SLOTS, PARTS)),
        ],
        compiler_params=grant(28),
        cost_estimate=small_cost(),
    )(slab, after)


STEP = 8


def ladder_body(last, base, place, bound, slab, mine, other, before, after, *rest):
    if last:
        o0, o1, o2, o3, amps, acc, folded, final = rest
    else:
        out, amps, acc, folded, final = rest
    y, core = place[0], place[3]
    _, rows, slots = slab.shape
    lanes = bound.shape[1]
    width = rows // (2 * CELLS)
    pairs = lanes // CELLS
    t_of = lax.broadcasted_iota(jnp.int32, (slots, lanes), 0)
    for s in range(mine.shape[0] // STEP):
        left, right = [], []
        for g in range(STEP):
            amps[g, :, pl.ds(core, 1)] = mine[s * STEP + g][:, None]
            amps[g, :, pl.ds(1 - core, 1)] = other[s * STEP + g][:, None]
            at = base + s * STEP + g
            edge = bound[at : at + 1, :]
            high, low = split(jnp.where(t_of < edge, amps[g].reshape(slots, lanes), 0.0))
            left.append(slab[at])
            right.append(jnp.concatenate([high, low], axis=1))
        part = jnp.dot(jnp.concatenate(left, axis=1), jnp.concatenate(right, axis=0), preferred_element_type=F32)
        if s == 0:
            acc[...] = part
        else:
            acc[...] += part
    half = rows // 2
    folded[...] = (acc[:half, :lanes] + acc[:half, lanes:]) + (acc[half:, :lanes] + acc[half:, lanes:])
    total = jnp.zeros((width, pairs), F32)
    for j in range(CELLS):
        total = total + folded[pl.ds(j, width, stride=CELLS), :][:, j * pairs : (j + 1) * pairs]
    total = total.T
    if not last:
        out[...] = total if base == 0 else total + before[...]
        return
    if base:
        total = total + before[...]
    final[...] = total
    own = pairs // 4
    for o, shift in ((o0, 0), (o1, 1), (o2, 3), (o3, 2)):
        o[...] = final[pl.ds(pl.multiple_of(lax.rem(y + shift, 4) * own, 8), own), :]


def ladder(place, bound, slab, mine, other, base, before, after, last):
    _, rows, slots = slab.shape
    lanes = bound.shape[1]
    pairs = lanes // CELLS
    width = rows // (2 * CELLS)
    if last:
        out_shape = (jax.ShapeDtypeStruct((pairs // 4, width), F32),) * 4
        out_specs = (vmem(),) * 4
    else:
        out_shape = jax.ShapeDtypeStruct((pairs, width), F32)
        out_specs = vmem()
    return pl.pallas_call(
        functools.partial(ladder_body, last, base),
        out_shape=out_shape,
        in_specs=[smem()] + [vmem()] * 5 + [anywhere()],
        out_specs=out_specs,
        scratch_shapes=[
            pltpu.VMEM((STEP, slots // 16, 2, 8, lanes), F32),
            pltpu.VMEM((rows, 2 * lanes), F32),
            pltpu.VMEM((rows // 2, lanes), F32),
            pltpu.VMEM((pairs, width), F32),
        ],
        compiler_params=grant(12),
        cost_estimate=small_cost(),
    )(place, bound, in_vmem(slab), mine, other, before, after)


def on_device(vir, occ, allowed, pair_list, occ_e, vir_e, ladder_amp, int_slab, cycle_amp, cycle_int):
    row, column = lax.axis_index("row"), lax.axis_index("column")
    place = jnp.stack(
        [lax.axis_index("depth"), row // 2, (row % 2) * 2 + column // 2, column % 2]
    ).astype(jnp.int32)
    pairs = ladder_amp.shape[0]
    width = int_slab.shape[1]
    own = pairs // 4

    mine = relayout(jnp.transpose(ladder_amp, (0, 2, 1)))
    blocks = [mine] + [send(mine, FIRST[n]) for n in (1, -1, 2)]
    choice = (pair_list[:, 1:] == jnp.arange(cycle_int.shape[1], dtype=jnp.int32)).astype(F32)
    choice = jnp.repeat(choice, cycle_amp.shape[1], axis=0)
    parts = cycle(place, cycle_amp, jnp.transpose(cycle_int, (1, 2, 0)), choice)
    line = stack(place, blocks, parts[0])
    pieces = [line] + [send(line, SECOND[n]) for n in (1, -1, 2)]
    bound, denom, live = labels(place, vir, occ, allowed, pair_list, occ_e, vir_e, width, own, pairs, line)
    keep, away = by_half(place, spread(parts, ALONG_Y), line)
    got = send(away, Z_ACROSS)
    slab, token = ready(in_hbm(int_slab.reshape(int_slab.shape[1:])), keep)

    chunks = pack(place, pieces, (token, got, bound))
    others = [send(v, SWAP) for v in chunks]
    parts = spread(by_row(place, keep, got, chunks[0]), ALONG_X)
    base, sums = 0, bound
    for i, count in enumerate(CHUNKS):
        sums = ladder(place, bound, slab, chunks[i], others[i], base, sums, parts[0], i == len(CHUNKS) - 1)
        base += count
    s0, s1, s2, s3 = spread(sums, ALONG_Y)
    total = (s0 + s1) + (s2 + s3) + (parts[0] + parts[1]) + (parts[2] + parts[3])
    return jnp.where(live > 0, total / denom, jnp.float32(0.0))[None]


def solution(mesh):
    return jax.shard_map(
        on_device,
        mesh=mesh,
        in_specs=(
            P(),
            P(),
            P(),
            P(),
            P(),
            P(),
            P(None, "depth", ("row", "column")),
            P("row", "column", "depth", None),
            P(None, None, ("depth", "row")),
            P(("depth", "row"), None, "column"),
        ),
        out_specs=P("row", "depth", "column"),
        check_vma=False,
    )
```

```python
import functools

import jax
import jax.numpy as jnp
from jax import lax
from jax.experimental import pallas as pl
from jax.experimental.pallas import tpu as pltpu
from jax.sharding import PartitionSpec as P

AXES = ("depth", "row", "column")
F32 = jnp.float32
BF16 = jnp.bfloat16
MIB = 1 << 20


def pairs_of(core0, core1):
    out = []
    for y in range(4):
        for x in range(4):
            for z in range(4):
                for k in range(2):
                    ty, tx, tz, tk = (core1 if k else core0)(y, x, z, k)
                    out.append((y * 32 + x * 8 + z * 2 + k, (ty % 4) * 32 + (tx % 4) * 8 + (tz % 4) * 2 + tk % 2))
    return out


def along_x(n):
    return lambda y, x, z, k: (y, x + n, z, k)


def along_y(n):
    return lambda y, x, z, k: (y + n, x, z, k)


def along_z(n):
    return lambda y, x, z, k: (y, x, z + n, k)


def other_core(y, x, z, k):
    return (y, x, z, k + 1)


FIRST = {n: pairs_of(along_x(n), along_z(n)) for n in (1, -1, 2)}
SECOND = {n: pairs_of(along_z(n), along_x(n)) for n in (1, -1, 2)}
ALONG_X = {n: pairs_of(along_x(n), along_x(n)) for n in (1, -1, 2)}
ALONG_Y = {n: pairs_of(along_y(n), along_y(n)) for n in (1, -1, 2)}
Z_ACROSS = pairs_of(along_z(2), along_z(2))
SWAP = pairs_of(other_core, other_core)


def send(value, pairs):
    return lax.ppermute(value, AXES, pairs)


def spread(parts, line):
    return (parts[0], send(parts[1], line[1]), send(parts[2], line[-1]), send(parts[3], line[2]))


def smem():
    return pl.BlockSpec(memory_space=pltpu.SMEM)


def vmem():
    return pl.BlockSpec(memory_space=pltpu.VMEM)


def anywhere():
    return pl.BlockSpec(memory_space=pl.ANY)


def in_vmem(value):
    return pltpu.with_memory_space_constraint(value, pltpu.VMEM)


def in_hbm(value):
    return pltpu.with_memory_space_constraint(value, pltpu.HBM)


def grant(mib):
    return pltpu.CompilerParams(vmem_limit_bytes=mib * MIB)


def small_cost():
    return pl.CostEstimate(flops=1, bytes_accessed=1, transcendentals=0)


CELLS = 4


def relayout_body(amp_ref, out_ref, turned):
    pairs, slots, cells = amp_ref.shape
    groups = cells // CELLS
    for t in range(slots):
        turned[t] = amp_ref[:, t, :].T
    for t in range(slots):
        pieces = [turned[t, pl.ds(j, groups, stride=CELLS), :] for j in range(CELLS)]
        out_ref[:, t, :] = jnp.concatenate(pieces, axis=1)


def relayout(amp):
    pairs, slots, cells = amp.shape
    return pl.pallas_call(
        relayout_body,
        out_shape=jax.ShapeDtypeStruct((cells // CELLS, slots, CELLS * pairs), F32),
        in_specs=[vmem()],
        out_specs=vmem(),
        scratch_shapes=[pltpu.VMEM((slots, cells, pairs), F32)],
        compiler_params=grant(8),
        cost_estimate=small_cost(),
    )(in_hbm(amp))


CHUNKS = (32, 32)


def stack_body(place, b0, b1, b2, b3, after, *out):
    own = jnp.where(place[3] == 0, place[1], place[2])
    base = 0
    for q in out:
        count = q.shape[0]
        for source, shift in ((b0, 0), (b1, 3), (b2, 1), (b3, 2)):
            q[:, pl.ds(lax.rem(own + shift, 4), 1)] = source[base : base + count][:, None]
        base += count


def stack(place, blocks, after):
    _, slots, lanes = blocks[0].shape
    return pl.pallas_call(
        stack_body,
        out_shape=tuple(jax.ShapeDtypeStruct((n, 4, slots, lanes), F32) for n in CHUNKS),
        in_specs=[smem()] + [vmem()] * 4 + [anywhere()],
        out_specs=(vmem(),) * len(CHUNKS),
        compiler_params=grant(8),
        cost_estimate=small_cost(),
    )(place, *blocks, after)


def pack_body(*refs):
    out = refs[-len(CHUNKS) :]
    for n, o in enumerate(out):
        for i in range(4):
            o[:, 4 * i : 4 * i + 4] = refs[4 * n + i][...]


def pack(held, after):
    _, _, slots, lanes = held[0][0].shape
    return pl.pallas_call(
        pack_body,
        out_shape=tuple(jax.ShapeDtypeStruct((n, 16, slots, lanes), F32) for n in CHUNKS),
        in_specs=[vmem()] * 4 * len(held) + [anywhere()] * len(after),
        out_specs=(vmem(),) * len(CHUNKS),
        compiler_params=grant(16),
        cost_estimate=small_cost(),
    )(*(p for pieces in held for p in pieces), *after)


def dot_nt(a, b):
    return lax.dot_general(a, b, (((1,), (1,)), ((), ())), preferred_element_type=F32)


def split(value):
    high = value.astype(BF16)
    return high, (value - high.astype(F32)).astype(BF16)


DEPTH_BLOCK = 1280


def cycle_body(depth, place, amp_ref, int_ref, choice_ref, keep, away, acc, by_row):
    step = pl.program_id(0)
    window, width, block = int_ref.shape
    pairs, rows, _ = amp_ref.shape

    @pl.when(step == 0)
    def _():
        acc[...] = jnp.zeros_like(acc)

    left = depth - step * block
    amp = amp_ref[...].reshape(pairs * rows, block)
    ints = int_ref[...].reshape(window * width, block)
    inside = lax.broadcasted_iota(jnp.int32, amp.shape, 1) < left
    high, low = split(jnp.where(inside, amp, 0.0))
    inside = lax.broadcasted_iota(jnp.int32, ints.shape, 1) < left
    int_high, int_low = split(jnp.where(inside, ints, 0.0))
    acc[...] += dot_nt(high, int_high) + dot_nt(high, int_low) + dot_nt(low, int_high)

    @pl.when(step == pl.num_programs(0) - 1)
    def _():
        total = jnp.zeros((pairs * rows, width), F32)
        for j in range(window):
            total = total + choice_ref[:, j : j + 1] * acc[:, j * width : (j + 1) * width]
        by_row[...] = total
        half = lax.div(place[2], 2)
        for x in range(rows // 2):
            keep[x] = by_row[pl.ds(2 * x + half, pairs, stride=rows), :]
            away[x] = by_row[pl.ds(2 * x + 1 - half, pairs, stride=rows), :]


def cycle(place, amp, ints, choice):
    pairs, rows, depth = amp.shape
    window, width, _ = ints.shape
    part = jax.ShapeDtypeStruct((rows // 2, pairs, width), F32)
    whole = pl.BlockSpec(part.shape, lambda i: (0, 0, 0))
    return pl.pallas_call(
        functools.partial(cycle_body, depth),
        grid=(pl.cdiv(depth, DEPTH_BLOCK),),
        out_shape=(part,) * 2,
        in_specs=[
            smem(),
            pl.BlockSpec((pairs, rows, DEPTH_BLOCK), lambda i: (0, 0, i)),
            pl.BlockSpec((window, width, DEPTH_BLOCK), lambda i: (0, 0, i)),
            pl.BlockSpec((pairs * rows, window), lambda i: (0, 0)),
        ],
        out_specs=(whole,) * 2,
        scratch_shapes=[
            pltpu.VMEM((pairs * rows, window * width), F32),
            pltpu.VMEM((pairs * rows, width), F32),
        ],
        compiler_params=grant(24),
        cost_estimate=small_cost(),
    )(place, in_hbm(amp), in_hbm(ints), choice)


def by_row_body(place, keep, got, after, o0, o1, o2, o3, held):
    held[...] = keep[...] + got[...]
    for out, shift in ((o0, 0), (o1, 1), (o2, 3), (o3, 2)):
        out[...] = held[lax.rem(place[1] + shift, 4)]


def by_row(place, keep, got, after):
    count, own, width = keep.shape
    return pl.pallas_call(
        by_row_body,
        out_shape=(jax.ShapeDtypeStruct((own, width), F32),) * 4,
        in_specs=[smem()] + [vmem()] * 2 + [anywhere()],
        out_specs=(vmem(),) * 4,
        scratch_shapes=[pltpu.VMEM((count, own, width), F32)],
        compiler_params=grant(8),
        cost_estimate=small_cost(),
    )(place, keep, got, after)


def labels(place, vir, occ, allowed, pair_list, occ_e, vir_e, vir_tile, bound, denom, live):
    y, x, z, core = place[0], place[1], place[2], place[3]
    row = x * 2 + lax.div(z, 2)
    column = lax.rem(z, 2) * 2 + core
    irreps = allowed.shape[0]
    total = vir.shape[0]
    pair_irrep = jnp.bitwise_xor(occ[pair_list[0, 0]], occ[pair_list[1, 0]])
    a_orb = row * 128
    ga = vir[a_orb]
    gb = jnp.bitwise_xor(ga, pair_irrep)
    tile = vir_tile[...]
    counts = [jnp.sum((tile == g).astype(jnp.int32)) for g in range(irreps)]
    starts = [jnp.int32(0)]
    for g in range(irreps - 1):
        starts.append(starts[g] + counts[g])
    count_b = jnp.int32(0)
    start_b = jnp.int32(0)
    groups, lanes = bound.shape
    cell = (
        y * (groups * CELLS)
        + lax.broadcasted_iota(jnp.int32, bound.shape, 0) * CELLS
        + lax.div(lax.broadcasted_iota(jnp.int32, bound.shape, 1), lanes // CELLS)
    )
    limit = jnp.zeros(bound.shape, jnp.int32)
    for g in range(irreps):
        count_b = jnp.where(gb == g, counts[g], count_b)
        start_b = jnp.where(gb == g, starts[g], start_b)
        partner = jnp.bitwise_xor(pair_irrep, g)
        reach = jnp.int32(0)
        for h in range(irreps):
            reach = jnp.where(partner == h, counts[h], reach)
        reach = reach * allowed[ga, gb, g]
        limit = jnp.where((cell >= starts[g]) & (cell < starts[g] + counts[g]), reach, limit)
    bound[...] = limit
    own, width = denom.shape
    slot = column * width + lax.broadcasted_iota(jnp.int32, (own, width), 1)
    line = lax.broadcasted_iota(jnp.int32, (own, width), 0)
    first = start_b + column * width

    def put(s, acc):
        orb = first + s
        value = jnp.where(orb < total, vir_e[jnp.minimum(orb, total - 1)], 0.0)
        return jnp.where(slot == column * width + s, value, acc)

    eps_b = lax.fori_loop(0, width, put, jnp.zeros((own, width), F32))
    eps_ij = jnp.zeros((own, width), F32)
    for p in range(own):
        i, j = pair_list[0, y * own + p], pair_list[1, y * own + p]
        eps_ij = jnp.where(line == p, occ_e[i] + occ_e[j], eps_ij)
    denom[...] = eps_ij - vir_e[a_orb] - eps_b
    live[...] = (slot < count_b).astype(jnp.int32)


READY = 4
SLOTS = 3
PARTS = 4


def ready_body(*refs):
    slab = refs[8]
    out, bound, denom, live, held, sems = refs[-6:]
    width, cells, slots = slab.shape
    steps = cells // (8 * READY)
    share = width // PARTS

    def copies(s):
        return [
            pltpu.make_async_copy(
                slab.at[pl.ds(n * share, share), pl.ds(s * READY * 8, READY * 8), :],
                held.at[s % SLOTS, pl.ds(n * share, share)],
                sems.at[s % SLOTS, n],
            )
            for n in range(PARTS)
        ]

    for s in range(SLOTS - 1):
        for c in copies(s):
            c.start()
    labels(*refs[:8], bound, denom, live)
    for s in range(steps):
        if s + SLOTS - 1 < steps:
            for c in copies(s + SLOTS - 1):
                c.start()
        for c in copies(s):
            c.wait()
        for g in range(READY):
            block = held[s % SLOTS, :, 8 * g : 8 * g + 8, :].reshape(width // 2, 2, 8, slots)
            even, odd = block[:, 0], block[:, 1]
            first = lax.broadcasted_iota(jnp.int32, even.shape, 1) < CELLS
            lower_cells = jnp.where(first, even, pltpu.roll(odd, CELLS, 1)).reshape(width * CELLS, slots)
            upper_cells = jnp.where(first, pltpu.roll(even, CELLS, 1), odd).reshape(width * CELLS, slots)
            for i, rows in enumerate((lower_cells, upper_cells)):
                at = (s * READY + g) * 2 + i
                high, low = split(rows)
                out[at, pl.ds(0, width * CELLS)] = high
                out[at, pl.ds(width * CELLS, width * CELLS)] = low


def ready(place, tables, vir_tile, slab, own, pairs, after):
    width, cells, slots = slab.shape
    return pl.pallas_call(
        ready_body,
        out_shape=(
            jax.ShapeDtypeStruct((cells // CELLS, 2 * CELLS * width, slots), BF16),
            jax.ShapeDtypeStruct((cells // CELLS, CELLS * pairs), jnp.int32),
            jax.ShapeDtypeStruct((own, width), F32),
            jax.ShapeDtypeStruct((own, width), jnp.int32),
        ),
        in_specs=[smem()] * 7 + [vmem()] + [anywhere()] * (1 + len(after)),
        out_specs=(vmem(),) * 4,
        scratch_shapes=[
            pltpu.VMEM((SLOTS, width, READY * 8, slots), F32),
            pltpu.SemaphoreType.DMA((SLOTS, PARTS)),
        ],
        compiler_params=grant(28),
        cost_estimate=small_cost(),
    )(place, *(in_hbm(v) for v in tables), vir_tile, in_hbm(slab), *after)


STEP = 8


def ladder_body(last, base, place, bound, slab, mine, other, before, after, *rest):
    if last:
        parts, rest = rest[:4], rest[4:]
        o0, o1, o2, o3, amps, acc, folded, final = rest
    else:
        out, amps, acc, folded, final = rest
    y, core = place[0], place[3]
    _, rows, slots = slab.shape
    lanes = bound.shape[1]
    width = rows // (2 * CELLS)
    pairs = lanes // CELLS
    x, z = place[1], place[2]
    tiles = []
    for source, at_first in ((mine, core == 0), (other, core == 1)):
        for n, shift in enumerate((0, 3, 1, 2)):
            first = jnp.where(at_first, lax.rem(z + shift, 4) * 2, lax.rem(x + shift, 4) * 8 + 1)
            for i in range(4):
                tiles.append((source, 4 * n + i, first + i * jnp.where(at_first, 8, 2)))
    t_of = lax.broadcasted_iota(jnp.int32, (slots, lanes), 0)
    for s in range(mine.shape[0] // STEP):
        left, right = [], []
        for g in range(STEP):
            for source, n, tile in tiles:
                amps[g, tile] = source[s * STEP + g, n]
            at = base + s * STEP + g
            edge = bound[at : at + 1, :]
            high, low = split(jnp.where(t_of < edge, amps[g].reshape(slots, lanes), 0.0))
            left.append(slab[at])
            right.append(jnp.concatenate([high, low], axis=1))
        part = jnp.dot(jnp.concatenate(left, axis=1), jnp.concatenate(right, axis=0), preferred_element_type=F32)
        if s == 0:
            acc[...] = part
        else:
            acc[...] += part
    half = rows // 2
    folded[...] = (acc[:half, :lanes] + acc[:half, lanes:]) + (acc[half:, :lanes] + acc[half:, lanes:])
    total = jnp.zeros((width, pairs), F32)
    for j in range(CELLS):
        total = total + folded[pl.ds(j, width, stride=CELLS), :][:, j * pairs : (j + 1) * pairs]
    total = total.T
    if not last:
        out[...] = total if base == 0 else total + before[...]
        return
    if base:
        total = total + before[...]
    final[...] = total + (parts[0][...] + parts[1][...]) + (parts[2][...] + parts[3][...])
    own = pairs // 4
    for o, shift in ((o0, 0), (o1, 1), (o2, 3), (o3, 2)):
        o[...] = final[pl.ds(pl.multiple_of(lax.rem(y + shift, 4) * own, 8), own), :]


def ladder(place, bound, slab, mine, other, base, before, after, parts=()):
    last = bool(parts)
    _, rows, slots = slab.shape
    lanes = bound.shape[1]
    pairs = lanes // CELLS
    width = rows // (2 * CELLS)
    if last:
        out_shape = (jax.ShapeDtypeStruct((pairs // 4, width), F32),) * 4
        out_specs = (vmem(),) * 4
    else:
        out_shape = jax.ShapeDtypeStruct((pairs, width), F32)
        out_specs = vmem()
    return pl.pallas_call(
        functools.partial(ladder_body, last, base),
        out_shape=out_shape,
        in_specs=[smem()] + [vmem()] * 5 + [anywhere()] + [vmem()] * len(parts),
        out_specs=out_specs,
        scratch_shapes=[
            pltpu.VMEM((STEP, slots // 8, 8, lanes), F32),
            pltpu.VMEM((rows, 2 * lanes), F32),
            pltpu.VMEM((rows // 2, lanes), F32),
            pltpu.VMEM((pairs, width), F32),
        ],
        compiler_params=grant(12),
        cost_estimate=small_cost(),
    )(place, bound, in_vmem(slab), mine, other, before, after, *parts)


def on_device(vir, occ, allowed, pair_list, occ_e, vir_e, ladder_amp, int_slab, cycle_amp, cycle_int):
    row, column = lax.axis_index("row"), lax.axis_index("column")
    place = jnp.stack(
        [lax.axis_index("depth"), row // 2, (row % 2) * 2 + column // 2, column % 2]
    ).astype(jnp.int32)
    pairs = ladder_amp.shape[0]
    width = int_slab.shape[1]
    own = pairs // 4

    mine = relayout(jnp.transpose(ladder_amp, (0, 2, 1)))
    blocks = [mine] + [send(mine, FIRST[n]) for n in (1, -1, 2)]
    choice = (pair_list[:, 1:] == jnp.arange(cycle_int.shape[1], dtype=jnp.int32)).astype(F32)
    choice = jnp.repeat(choice, cycle_amp.shape[1], axis=0)
    keep, away = cycle(place, cycle_amp, jnp.transpose(cycle_int, (1, 2, 0)), choice)
    low, high = stack(place, blocks, keep)
    low_below, high_above = send(low, SECOND[1]), send(high, SECOND[-1])
    high_below, low_above = send(high, SECOND[1]), send(low, SECOND[-1])
    got = send(away, Z_ACROSS)
    slab, bound, denom, live = ready(
        place,
        (vir, occ, allowed, pair_list.T, occ_e, vir_e),
        vir.reshape(8, -1),
        int_slab.reshape(int_slab.shape[1:]),
        own,
        pairs,
        (low_below, high_above),
    )
    held = [
        (low, low_below, low_above, send(low_below, SECOND[1])),
        (high, high_below, high_above, send(high_above, SECOND[-1])),
    ]
    chunks = pack(held, (bound, got))
    others = [send(v, SWAP) for v in chunks]
    parts = spread(by_row(place, keep, got, chunks[0]), ALONG_X)
    sums = ladder(place, bound, slab, chunks[0], others[0], 0, bound, bound)
    sums = ladder(place, bound, slab, chunks[1], others[1], CHUNKS[0], sums, bound, parts)
    s0, s1, s2, s3 = spread(sums, ALONG_Y)
    total = (s0 + s1) + (s2 + s3)
    return jnp.where(live > 0, total / denom, jnp.float32(0.0))[None]


def solution(mesh):
    return jax.shard_map(
        on_device,
        mesh=mesh,
        in_specs=(
            P(),
            P(),
            P(),
            P(),
            P(),
            P(),
            P(None, "depth", ("row", "column")),
            P("row", "column", "depth", None),
            P(None, None, ("depth", "row")),
            P(("depth", "row"), None, "column"),
        ),
        out_specs=P("row", "depth", "column"),
        check_vma=False,
    )
```

```python
import functools

import jax
import jax.numpy as jnp
from jax import lax
from jax.experimental import pallas as pl
from jax.experimental.pallas import tpu as pltpu
from jax.sharding import PartitionSpec as P

AXES = ("depth", "row", "column")
F32 = jnp.float32
BF16 = jnp.bfloat16
MIB = 1 << 20


def pairs_of(core0, core1):
    out = []
    for y in range(4):
        for x in range(4):
            for z in range(4):
                for k in range(2):
                    ty, tx, tz, tk = (core1 if k else core0)(y, x, z, k)
                    out.append((y * 32 + x * 8 + z * 2 + k, (ty % 4) * 32 + (tx % 4) * 8 + (tz % 4) * 2 + tk % 2))
    return out


def along_x(n):
    return lambda y, x, z, k: (y, x + n, z, k)


def along_y(n):
    return lambda y, x, z, k: (y + n, x, z, k)


def along_z(n):
    return lambda y, x, z, k: (y, x, z + n, k)


def other_core(y, x, z, k):
    return (y, x, z, k + 1)


FIRST = {n: pairs_of(along_x(n), along_z(n)) for n in (1, -1, 2)}
SECOND = {n: pairs_of(along_z(n), along_x(n)) for n in (1, -1, 2)}
ALONG_Y = {n: pairs_of(along_y(n), along_y(n)) for n in (1, -1, 2)}
SWAP = pairs_of(other_core, other_core)


def send(value, pairs):
    return lax.ppermute(value, AXES, pairs)


def spread(parts, line):
    return (parts[0], send(parts[1], line[1]), send(parts[2], line[-1]), send(parts[3], line[2]))


def smem():
    return pl.BlockSpec(memory_space=pltpu.SMEM)


def vmem():
    return pl.BlockSpec(memory_space=pltpu.VMEM)


def anywhere():
    return pl.BlockSpec(memory_space=pl.ANY)


def in_vmem(value):
    return pltpu.with_memory_space_constraint(value, pltpu.VMEM)


def in_hbm(value):
    return pltpu.with_memory_space_constraint(value, pltpu.HBM)


def grant(mib):
    return pltpu.CompilerParams(vmem_limit_bytes=mib * MIB)


def small_cost():
    return pl.CostEstimate(flops=1, bytes_accessed=1, transcendentals=0)


CELLS = 4


def relayout_body(amp_ref, out_ref, turned):
    pairs, slots, cells = amp_ref.shape
    groups = cells // CELLS
    for t in range(slots):
        turned[t] = amp_ref[:, t, :].T
    for t in range(slots):
        pieces = [turned[t, pl.ds(j, groups, stride=CELLS), :] for j in range(CELLS)]
        out_ref[:, t, :] = jnp.concatenate(pieces, axis=1)


def relayout(amp):
    pairs, slots, cells = amp.shape
    return pl.pallas_call(
        relayout_body,
        out_shape=jax.ShapeDtypeStruct((cells // CELLS, slots, CELLS * pairs), F32),
        in_specs=[vmem()],
        out_specs=vmem(),
        scratch_shapes=[pltpu.VMEM((slots, cells, pairs), F32)],
        compiler_params=grant(8),
        cost_estimate=small_cost(),
    )(in_hbm(amp))


CHUNKS = (32, 32)


def stack_body(place, b0, b1, b2, b3, share, *out):
    own = jnp.where(place[3] == 0, place[1], place[2])
    base = 0
    extra = share.shape[0] // len(CHUNKS)
    for n, (q, count) in enumerate(zip(out, CHUNKS)):
        for source, shift in ((b0, 0), (b1, 3), (b2, 1), (b3, 2)):
            q[0:count, pl.ds(lax.rem(own + shift, 4), 1)] = source[base : base + count][:, None]
        q[count:] = share[n * extra : (n + 1) * extra]
        base += count


def stack(place, blocks, share):
    _, slots, lanes = blocks[0].shape
    sizes = [n + share.shape[0] // len(CHUNKS) for n in CHUNKS]
    return pl.pallas_call(
        stack_body,
        out_shape=tuple(jax.ShapeDtypeStruct((n, 4, slots, lanes), F32) for n in sizes),
        in_specs=[smem()] + [vmem()] * 5,
        out_specs=(vmem(),) * len(CHUNKS),
        compiler_params=grant(8),
        cost_estimate=small_cost(),
    )(place, *blocks, share)


def pack_body(*refs):
    out = refs[-len(CHUNKS) :]
    for n, o in enumerate(out):
        for i in range(4):
            o[:, 4 * i : 4 * i + 4] = refs[4 * n + i][0 : CHUNKS[n]]


def pack(held, after):
    _, _, slots, lanes = held[0][0].shape
    return pl.pallas_call(
        pack_body,
        out_shape=tuple(jax.ShapeDtypeStruct((n, 16, slots, lanes), F32) for n in CHUNKS),
        in_specs=[vmem()] * 4 * len(held) + [anywhere()] * len(after),
        out_specs=(vmem(),) * len(CHUNKS),
        compiler_params=grant(16),
        cost_estimate=small_cost(),
    )(*(p for pieces in held for p in pieces), *after)


def dot_nt(a, b):
    return lax.dot_general(a, b, (((1,), (1,)), ((), ())), preferred_element_type=F32)


def split(value):
    high = value.astype(BF16)
    return high, (value - high.astype(F32)).astype(BF16)


DEPTH_BLOCK = 2432


def cycle_body(depth, place, amp_ref, int_ref, choice_ref, out, acc, by_row):
    step = pl.program_id(0)
    window, width, block = int_ref.shape
    pairs, rows, _ = amp_ref.shape

    @pl.when(step == 0)
    def _():
        acc[...] = jnp.zeros_like(acc)

    left = depth - step * block
    amp = amp_ref[...].reshape(pairs * rows, block)
    ints = int_ref[...].reshape(window * width, block)
    inside = lax.broadcasted_iota(jnp.int32, amp.shape, 1) < left
    high, low = split(jnp.where(inside, amp, 0.0))
    inside = lax.broadcasted_iota(jnp.int32, ints.shape, 1) < left
    int_high, int_low = split(jnp.where(inside, ints, 0.0))
    acc[...] += dot_nt(high, int_high) + dot_nt(high, int_low) + dot_nt(low, int_high)

    @pl.when(step == pl.num_programs(0) - 1)
    def _():
        total = jnp.zeros((pairs * rows, width), F32)
        for j in range(window):
            total = total + choice_ref[:, j : j + 1] * acc[:, j * width : (j + 1) * width]
        by_row[...] = total
        for x in range(rows // 2):
            pair = [by_row[pl.ds(2 * x + h, pairs, stride=rows), :] for h in range(2)]
            out[x] = jnp.concatenate(pair, axis=1).reshape(pairs // 8, 8, 2 * width)


def cycle(place, amp, ints, choice):
    pairs, rows, depth = amp.shape
    window, width, _ = ints.shape
    part = jax.ShapeDtypeStruct((rows // 2, pairs // 8, 8, 2 * width), F32)
    whole = pl.BlockSpec(part.shape, lambda i: (0, 0, 0, 0))
    return pl.pallas_call(
        functools.partial(cycle_body, depth),
        grid=(pl.cdiv(depth, DEPTH_BLOCK),),
        out_shape=part,
        in_specs=[
            smem(),
            pl.BlockSpec((pairs, rows, DEPTH_BLOCK), lambda i: (0, 0, i)),
            pl.BlockSpec((window, width, DEPTH_BLOCK), lambda i: (0, 0, i)),
            pl.BlockSpec((pairs * rows, window), lambda i: (0, 0)),
        ],
        out_specs=whole,
        scratch_shapes=[
            pltpu.VMEM((pairs * rows, window * width), F32),
            pltpu.VMEM((pairs * rows, width), F32),
        ],
        compiler_params=grant(24),
        cost_estimate=small_cost(),
    )(place, in_hbm(amp), in_hbm(ints), choice)


def shares_body(place, *refs):
    o0, o1, o2, o3, far, near = refs[-6:]
    x, half, core = place[1], lax.div(place[2], 2), place[3]
    window, _, slots, lanes = far.shape
    pairs, width = o0.shape
    extra = window // len(CHUNKS)
    for n, first in enumerate(CHUNKS):
        own, below, above, across = refs[4 * n : 4 * n + 4]
        part = slice(n * extra, (n + 1) * extra)
        far[part] = own[first:] + across[first:]
        near[part] = below[first:] + above[first:]

    def side(value, which):
        value = value.reshape(pairs, lanes)
        return jnp.where(which == 0, value[:, :width], value[:, width:])

    @pl.when(core == 0)
    def _():
        for out, shift in ((o0, 0), (o1, 1), (o2, 3), (o3, 2)):
            out[...] = side(far[lax.rem(x + shift, 4)], half)

    @pl.when(core == 1)
    def _():
        total = far[x] + near[x]
        o0[...] = side(total, half)
        o1[...] = jnp.zeros_like(o1)
        o2[...] = jnp.zeros_like(o2)
        o3[...] = side(total, 1 - half)


def shares(place, held, pairs, width, after):
    extra, _, slots, lanes = held[0][0].shape
    extra = (extra - CHUNKS[0]) * len(CHUNKS)
    return pl.pallas_call(
        shares_body,
        out_shape=(jax.ShapeDtypeStruct((pairs, width), F32),) * 4,
        in_specs=[smem()] + [vmem()] * 4 * len(held) + [anywhere()],
        out_specs=(vmem(),) * 4,
        scratch_shapes=[pltpu.VMEM((extra, 4, slots, lanes), F32)] * 2,
        compiler_params=grant(16),
        cost_estimate=small_cost(),
    )(place, *(p for pieces in held for p in pieces), after)


def labels(place, vir, occ, allowed, pair_list, occ_e, vir_e, vir_tile, bound, denom, live):
    y, x, z, core = place[0], place[1], place[2], place[3]
    row = x * 2 + lax.div(z, 2)
    column = lax.rem(z, 2) * 2 + core
    irreps = allowed.shape[0]
    total = vir.shape[0]
    pair_irrep = jnp.bitwise_xor(occ[pair_list[0, 0]], occ[pair_list[1, 0]])
    a_orb = row * 128
    ga = vir[a_orb]
    gb = jnp.bitwise_xor(ga, pair_irrep)
    tile = vir_tile[...]
    counts = [jnp.sum((tile == g).astype(jnp.int32)) for g in range(irreps)]
    starts = [jnp.int32(0)]
    for g in range(irreps - 1):
        starts.append(starts[g] + counts[g])
    count_b = jnp.int32(0)
    start_b = jnp.int32(0)
    groups, lanes = bound.shape
    cell = (
        y * (groups * CELLS)
        + lax.broadcasted_iota(jnp.int32, bound.shape, 0) * CELLS
        + lax.div(lax.broadcasted_iota(jnp.int32, bound.shape, 1), lanes // CELLS)
    )
    limit = jnp.zeros(bound.shape, jnp.int32)
    for g in range(irreps):
        count_b = jnp.where(gb == g, counts[g], count_b)
        start_b = jnp.where(gb == g, starts[g], start_b)
        partner = jnp.bitwise_xor(pair_irrep, g)
        reach = jnp.int32(0)
        for h in range(irreps):
            reach = jnp.where(partner == h, counts[h], reach)
        reach = reach * allowed[ga, gb, g]
        limit = jnp.where((cell >= starts[g]) & (cell < starts[g] + counts[g]), reach, limit)
    bound[...] = limit
    own, width = denom.shape
    slot = column * width + lax.broadcasted_iota(jnp.int32, (own, width), 1)
    line = lax.broadcasted_iota(jnp.int32, (own, width), 0)
    first = start_b + column * width

    def put(s, acc):
        orb = first + s
        value = jnp.where(orb < total, vir_e[jnp.minimum(orb, total - 1)], 0.0)
        return jnp.where(slot == column * width + s, value, acc)

    eps_b = lax.fori_loop(0, width, put, jnp.zeros((own, width), F32), unroll=8)
    eps_ij = jnp.zeros((own, width), F32)
    for p in range(own):
        i, j = pair_list[0, y * own + p], pair_list[1, y * own + p]
        eps_ij = jnp.where(line == p, occ_e[i] + occ_e[j], eps_ij)
    denom[...] = eps_ij - vir_e[a_orb] - eps_b
    live[...] = (slot < count_b).astype(jnp.int32)


READY = 4
SLOTS = 4
PARTS = 4


def ready_body(*refs):
    slab = refs[8]
    out, bound, denom, live, held, sems = refs[-6:]
    width, cells, slots = slab.shape
    steps = cells // (8 * READY)
    share = width // PARTS

    def copies(s):
        return [
            pltpu.make_async_copy(
                slab.at[pl.ds(n * share, share), pl.ds(s * READY * 8, READY * 8), :],
                held.at[s % SLOTS, pl.ds(n * share, share)],
                sems.at[s % SLOTS, n],
            )
            for n in range(PARTS)
        ]

    for s in range(SLOTS - 1):
        for c in copies(s):
            c.start()
    labels(*refs[:8], bound, denom, live)
    for s in range(steps):
        if s + SLOTS - 1 < steps:
            for c in copies(s + SLOTS - 1):
                c.start()
        for c in copies(s):
            c.wait()
        for g in range(READY):
            block = held[s % SLOTS, :, 8 * g : 8 * g + 8, :].reshape(width // 2, 2, 8, slots)
            even, odd = block[:, 0], block[:, 1]
            first = lax.broadcasted_iota(jnp.int32, even.shape, 1) < CELLS
            lower_cells = jnp.where(first, even, pltpu.roll(odd, CELLS, 1)).reshape(width * CELLS, slots)
            upper_cells = jnp.where(first, pltpu.roll(even, CELLS, 1), odd).reshape(width * CELLS, slots)
            for i, rows in enumerate((lower_cells, upper_cells)):
                at = (s * READY + g) * 2 + i
                high, low = split(rows)
                out[at, pl.ds(0, width * CELLS)] = high
                out[at, pl.ds(width * CELLS, width * CELLS)] = low


def ready(place, tables, vir_tile, slab, own, pairs, after):
    width, cells, slots = slab.shape
    return pl.pallas_call(
        ready_body,
        out_shape=(
            jax.ShapeDtypeStruct((cells // CELLS, 2 * CELLS * width, slots), BF16),
            jax.ShapeDtypeStruct((cells // CELLS, CELLS * pairs), jnp.int32),
            jax.ShapeDtypeStruct((own, width), F32),
            jax.ShapeDtypeStruct((own, width), jnp.int32),
        ),
        in_specs=[smem()] * 7 + [vmem()] + [anywhere()] * (1 + len(after)),
        out_specs=(vmem(),) * 4,
        scratch_shapes=[
            pltpu.VMEM((SLOTS, width, READY * 8, slots), F32),
            pltpu.SemaphoreType.DMA((SLOTS, PARTS)),
        ],
        compiler_params=grant(28),
        cost_estimate=small_cost(),
    )(place, *(in_hbm(v) for v in tables), vir_tile, in_hbm(slab), *after)


STEP = 8


def ladder_body(last, base, place, bound, slab, mine, other, before, after, *rest):
    if last:
        parts, rest = rest[:4], rest[4:]
        o0, o1, o2, o3, amps, acc, folded, final = rest
    else:
        out, amps, acc, folded, final = rest
    y, core = place[0], place[3]
    _, rows, slots = slab.shape
    lanes = bound.shape[1]
    width = rows // (2 * CELLS)
    pairs = lanes // CELLS
    x, z = place[1], place[2]
    tiles = []
    for source, at_first in ((mine, core == 0), (other, core == 1)):
        for n, shift in enumerate((0, 3, 1, 2)):
            first = jnp.where(at_first, lax.rem(z + shift, 4) * 2, lax.rem(x + shift, 4) * 8 + 1)
            for i in range(4):
                tiles.append((source, 4 * n + i, first + i * jnp.where(at_first, 8, 2)))
    t_of = lax.broadcasted_iota(jnp.int32, (slots, lanes), 0)
    for s in range(mine.shape[0] // STEP):
        left, right = [], []
        for g in range(STEP):
            for source, n, tile in tiles:
                amps[g, tile] = source[s * STEP + g, n]
            at = base + s * STEP + g
            edge = bound[at : at + 1, :]
            high, low = split(jnp.where(t_of < edge, amps[g].reshape(slots, lanes), 0.0))
            left.append(slab[at])
            right.append(jnp.concatenate([high, low], axis=1))
        part = jnp.dot(jnp.concatenate(left, axis=1), jnp.concatenate(right, axis=0), preferred_element_type=F32)
        if s == 0:
            acc[...] = part
        else:
            acc[...] += part
    half = rows // 2
    folded[...] = (acc[:half, :lanes] + acc[:half, lanes:]) + (acc[half:, :lanes] + acc[half:, lanes:])
    total = jnp.zeros((width, pairs), F32)
    for j in range(CELLS):
        total = total + folded[pl.ds(j, width, stride=CELLS), :][:, j * pairs : (j + 1) * pairs]
    total = total.T
    if not last:
        out[...] = total if base == 0 else total + before[...]
        return
    if base:
        total = total + before[...]
    final[...] = total + (parts[0][...] + parts[1][...]) + (parts[2][...] + parts[3][...])
    own = pairs // 4
    for o, shift in ((o0, 0), (o1, 1), (o2, 3), (o3, 2)):
        o[...] = final[pl.ds(pl.multiple_of(lax.rem(y + shift, 4) * own, 8), own), :]


def ladder(place, bound, slab, mine, other, base, before, after, parts=()):
    last = bool(parts)
    _, rows, slots = slab.shape
    lanes = bound.shape[1]
    pairs = lanes // CELLS
    width = rows // (2 * CELLS)
    if last:
        out_shape = (jax.ShapeDtypeStruct((pairs // 4, width), F32),) * 4
        out_specs = (vmem(),) * 4
    else:
        out_shape = jax.ShapeDtypeStruct((pairs, width), F32)
        out_specs = vmem()
    return pl.pallas_call(
        functools.partial(ladder_body, last, base),
        out_shape=out_shape,
        in_specs=[smem()] + [vmem()] * 5 + [anywhere()] + [vmem()] * len(parts),
        out_specs=out_specs,
        scratch_shapes=[
            pltpu.VMEM((STEP, slots // 8, 8, lanes), F32),
            pltpu.VMEM((rows, 2 * lanes), F32),
            pltpu.VMEM((rows // 2, lanes), F32),
            pltpu.VMEM((pairs, width), F32),
        ],
        compiler_params=grant(12),
        cost_estimate=small_cost(),
    )(place, bound, in_vmem(slab), mine, other, before, after, *parts)


def on_device(vir, occ, allowed, pair_list, occ_e, vir_e, ladder_amp, int_slab, cycle_amp, cycle_int):
    row, column = lax.axis_index("row"), lax.axis_index("column")
    place = jnp.stack(
        [lax.axis_index("depth"), row // 2, (row % 2) * 2 + column // 2, column % 2]
    ).astype(jnp.int32)
    pairs = ladder_amp.shape[0]
    width = int_slab.shape[1]
    own = pairs // 4

    mine = relayout(jnp.transpose(ladder_amp, (0, 2, 1)))
    blocks = [mine] + [send(mine, FIRST[n]) for n in (1, -1, 2)]
    choice = (pair_list[:, 1:] == jnp.arange(cycle_int.shape[1], dtype=jnp.int32)).astype(F32)
    choice = jnp.repeat(choice, cycle_amp.shape[1], axis=0)
    share = cycle(place, cycle_amp, jnp.transpose(cycle_int, (1, 2, 0)), choice)
    low, high = stack(place, blocks, share)
    low_below, high_above = send(low, SECOND[1]), send(high, SECOND[-1])
    high_below, low_above = send(high, SECOND[1]), send(low, SECOND[-1])
    slab, bound, denom, live = ready(
        place,
        (vir, occ, allowed, pair_list.T, occ_e, vir_e),
        vir.reshape(8, -1),
        int_slab.reshape(int_slab.shape[1:]),
        own,
        pairs,
        (low_below, high_above),
    )
    held = [
        (low, low_below, low_above, send(low_below, SECOND[1])),
        (high, high_below, high_above, send(high_above, SECOND[-1])),
    ]
    chunks = pack(held, (bound,))
    others = [send(v, SWAP) for v in chunks]
    parts = spread(shares(place, held, pairs, width, chunks[0]), FIRST)
    sums = ladder(place, bound, slab, chunks[0], others[0], 0, bound, bound)
    sums = ladder(place, bound, slab, chunks[1], others[1], CHUNKS[0], sums, bound, parts)
    s0, s1, s2, s3 = spread(sums, ALONG_Y)
    total = (s0 + s1) + (s2 + s3)
    return jnp.where(live > 0, total / denom, jnp.float32(0.0))[None]


def solution(mesh):
    return jax.shard_map(
        on_device,
        mesh=mesh,
        in_specs=(
            P(),
            P(),
            P(),
            P(),
            P(),
            P(),
            P(None, "depth", ("row", "column")),
            P("row", "column", "depth", None),
            P(None, None, ("depth", "row")),
            P(("depth", "row"), None, "column"),
        ),
        out_specs=P("row", "depth", "column"),
        check_vma=False,
    )
```

```python
import functools

import jax
import jax.numpy as jnp
from jax import lax
from jax.experimental import pallas as pl
from jax.experimental.pallas import tpu as pltpu
from jax.sharding import PartitionSpec as P

AXES = ("depth", "row", "column")
F32 = jnp.float32
BF16 = jnp.bfloat16
MIB = 1 << 20


def pairs_of(core0, core1):
    out = []
    for y in range(4):
        for x in range(4):
            for z in range(4):
                for k in range(2):
                    ty, tx, tz, tk = (core1 if k else core0)(y, x, z, k)
                    out.append((y * 32 + x * 8 + z * 2 + k, (ty % 4) * 32 + (tx % 4) * 8 + (tz % 4) * 2 + tk % 2))
    return out


def along_x(n):
    return lambda y, x, z, k: (y, x + n, z, k)


def along_y(n):
    return lambda y, x, z, k: (y + n, x, z, k)


def along_z(n):
    return lambda y, x, z, k: (y, x, z + n, k)


def other_core(y, x, z, k):
    return (y, x, z, k + 1)


FIRST = {n: pairs_of(along_x(n), along_z(n)) for n in (1, -1, 2)}
SECOND = {n: pairs_of(along_z(n), along_x(n)) for n in (1, -1, 2)}
ALONG_Y = {n: pairs_of(along_y(n), along_y(n)) for n in (1, -1, 2)}
SWAP = pairs_of(other_core, other_core)


def send(value, pairs):
    return lax.ppermute(value, AXES, pairs)


def spread(parts, line):
    return (parts[0], send(parts[1], line[1]), send(parts[2], line[-1]), send(parts[3], line[2]))


def smem():
    return pl.BlockSpec(memory_space=pltpu.SMEM)


def vmem():
    return pl.BlockSpec(memory_space=pltpu.VMEM)


def anywhere():
    return pl.BlockSpec(memory_space=pl.ANY)


def in_vmem(value):
    return pltpu.with_memory_space_constraint(value, pltpu.VMEM)


def in_hbm(value):
    return pltpu.with_memory_space_constraint(value, pltpu.HBM)


def grant(mib):
    return pltpu.CompilerParams(vmem_limit_bytes=mib * MIB)


def small_cost():
    return pl.CostEstimate(flops=1, bytes_accessed=1, transcendentals=0)


CELLS = 4


def relayout_body(amp_ref, out_ref, turned):
    pairs, slots, cells = amp_ref.shape
    groups = cells // CELLS
    for t in range(slots):
        turned[t] = amp_ref[:, t, :].T
    for t in range(slots):
        pieces = [turned[t, pl.ds(j, groups, stride=CELLS), :] for j in range(CELLS)]
        out_ref[:, t, :] = jnp.concatenate(pieces, axis=1)


def relayout(amp):
    pairs, slots, cells = amp.shape
    return pl.pallas_call(
        relayout_body,
        out_shape=jax.ShapeDtypeStruct((cells // CELLS, slots, CELLS * pairs), F32),
        in_specs=[vmem()],
        out_specs=vmem(),
        scratch_shapes=[pltpu.VMEM((slots, cells, pairs), F32)],
        compiler_params=grant(8),
        cost_estimate=small_cost(),
    )(in_hbm(amp))


CHUNKS = (32, 32)


def stack_body(place, b0, b1, b2, b3, share, *out):
    own = jnp.where(place[3] == 0, place[1], place[2])
    base = 0
    extra = share.shape[0] // len(CHUNKS)
    for n, (q, count) in enumerate(zip(out, CHUNKS)):
        for source, shift in ((b0, 0), (b1, 3), (b2, 1), (b3, 2)):
            q[0:count, pl.ds(lax.rem(own + shift, 4), 1)] = source[base : base + count][:, None]
        q[count:] = share[n * extra : (n + 1) * extra]
        base += count


def stack(place, blocks, share):
    _, slots, lanes = blocks[0].shape
    sizes = [n + share.shape[0] // len(CHUNKS) for n in CHUNKS]
    return pl.pallas_call(
        stack_body,
        out_shape=tuple(jax.ShapeDtypeStruct((n, 4, slots, lanes), F32) for n in sizes),
        in_specs=[smem()] + [vmem()] * 5,
        out_specs=(vmem(),) * len(CHUNKS),
        compiler_params=grant(8),
        cost_estimate=small_cost(),
    )(place, *blocks, share)


def pack_body(place, *refs):
    for n, o in enumerate(refs[-8:-6]):
        for i in range(4):
            o[:, 4 * i : 4 * i + 4] = refs[4 * n + i][0 : CHUNKS[n]]
    shares_body(place, *refs[:8], *refs[-6:])


def pack(place, held, pairs, width, after):
    extra, _, slots, lanes = held[0][0].shape
    extra = (extra - CHUNKS[0]) * len(CHUNKS)
    return pl.pallas_call(
        pack_body,
        out_shape=tuple(jax.ShapeDtypeStruct((n, 16, slots, lanes), F32) for n in CHUNKS)
        + (jax.ShapeDtypeStruct((pairs, width), F32),) * 4,
        in_specs=[smem()] + [vmem()] * 4 * len(held) + [anywhere()] * len(after),
        out_specs=(vmem(),) * (len(CHUNKS) + 4),
        scratch_shapes=[pltpu.VMEM((extra, 4, slots, lanes), F32)] * 2,
        compiler_params=grant(16),
        cost_estimate=small_cost(),
    )(place, *(p for pieces in held for p in pieces), *after)


def dot_nt(a, b):
    return lax.dot_general(a, b, (((1,), (1,)), ((), ())), preferred_element_type=F32)


def split(value):
    high = value.astype(BF16)
    return high, (value - high.astype(F32)).astype(BF16)


DEPTH_BLOCK = 2432


def cycle_body(depth, place, amp_ref, int_ref, choice_ref, out, acc, by_row):
    step = pl.program_id(0)
    window, width, block = int_ref.shape
    pairs, rows, _ = amp_ref.shape

    @pl.when(step == 0)
    def _():
        acc[...] = jnp.zeros_like(acc)

    left = depth - step * block
    amp = amp_ref[...].reshape(pairs * rows, block)
    ints = int_ref[...].reshape(window * width, block)
    inside = lax.broadcasted_iota(jnp.int32, amp.shape, 1) < left
    high, low = split(jnp.where(inside, amp, 0.0))
    inside = lax.broadcasted_iota(jnp.int32, ints.shape, 1) < left
    int_high, int_low = split(jnp.where(inside, ints, 0.0))
    acc[...] += dot_nt(high, int_high) + dot_nt(high, int_low) + dot_nt(low, int_high)

    @pl.when(step == pl.num_programs(0) - 1)
    def _():
        total = jnp.zeros((pairs * rows, width), F32)
        for j in range(window):
            total = total + choice_ref[:, j : j + 1] * acc[:, j * width : (j + 1) * width]
        by_row[...] = total
        for x in range(rows // 2):
            pair = [by_row[pl.ds(2 * x + h, pairs, stride=rows), :] for h in range(2)]
            out[x] = jnp.concatenate(pair, axis=1).reshape(pairs // 8, 8, 2 * width)


def cycle(place, amp, ints, choice):
    pairs, rows, depth = amp.shape
    window, width, _ = ints.shape
    part = jax.ShapeDtypeStruct((rows // 2, pairs // 8, 8, 2 * width), F32)
    whole = pl.BlockSpec(part.shape, lambda i: (0, 0, 0, 0))
    return pl.pallas_call(
        functools.partial(cycle_body, depth),
        grid=(pl.cdiv(depth, DEPTH_BLOCK),),
        out_shape=part,
        in_specs=[
            smem(),
            pl.BlockSpec((pairs, rows, DEPTH_BLOCK), lambda i: (0, 0, i)),
            pl.BlockSpec((window, width, DEPTH_BLOCK), lambda i: (0, 0, i)),
            pl.BlockSpec((pairs * rows, window), lambda i: (0, 0)),
        ],
        out_specs=whole,
        scratch_shapes=[
            pltpu.VMEM((pairs * rows, window * width), F32),
            pltpu.VMEM((pairs * rows, width), F32),
        ],
        compiler_params=grant(24),
        cost_estimate=small_cost(),
    )(place, in_hbm(amp), in_hbm(ints), choice)


def shares_body(place, *refs):
    o0, o1, o2, o3, far, near = refs[-6:]
    x, half, core = place[1], lax.div(place[2], 2), place[3]
    window, _, slots, lanes = far.shape
    pairs, width = o0.shape
    extra = window // len(CHUNKS)
    for n, first in enumerate(CHUNKS):
        own, below, above, across = refs[4 * n : 4 * n + 4]
        part = slice(n * extra, (n + 1) * extra)
        far[part] = own[first:] + across[first:]
        near[part] = below[first:] + above[first:]

    def side(value, which):
        value = value.reshape(pairs, lanes)
        return jnp.where(which == 0, value[:, :width], value[:, width:])

    @pl.when(core == 0)
    def _():
        for out, shift in ((o0, 0), (o1, 1), (o2, 3), (o3, 2)):
            out[...] = side(far[lax.rem(x + shift, 4)], half)

    @pl.when(core == 1)
    def _():
        total = far[x] + near[x]
        o0[...] = side(total, half)
        o1[...] = jnp.zeros_like(o1)
        o2[...] = jnp.zeros_like(o2)
        o3[...] = side(total, 1 - half)


def labels(place, vir, occ, allowed, pair_list, occ_e, vir_e, vir_tile, bound, denom, live):
    y, x, z, core = place[0], place[1], place[2], place[3]
    row = x * 2 + lax.div(z, 2)
    column = lax.rem(z, 2) * 2 + core
    irreps = allowed.shape[0]
    total = vir.shape[0]
    pair_irrep = jnp.bitwise_xor(occ[pair_list[0, 0]], occ[pair_list[1, 0]])
    a_orb = row * 128
    ga = vir[a_orb]
    gb = jnp.bitwise_xor(ga, pair_irrep)
    tile = vir_tile[...]
    counts = [jnp.sum((tile == g).astype(jnp.int32)) for g in range(irreps)]
    starts = [jnp.int32(0)]
    for g in range(irreps - 1):
        starts.append(starts[g] + counts[g])
    count_b = jnp.int32(0)
    start_b = jnp.int32(0)
    groups, lanes = bound.shape
    cell = (
        y * (groups * CELLS)
        + lax.broadcasted_iota(jnp.int32, bound.shape, 0) * CELLS
        + lax.div(lax.broadcasted_iota(jnp.int32, bound.shape, 1), lanes // CELLS)
    )
    limit = jnp.zeros(bound.shape, jnp.int32)
    for g in range(irreps):
        count_b = jnp.where(gb == g, counts[g], count_b)
        start_b = jnp.where(gb == g, starts[g], start_b)
        partner = jnp.bitwise_xor(pair_irrep, g)
        reach = jnp.int32(0)
        for h in range(irreps):
            reach = jnp.where(partner == h, counts[h], reach)
        reach = reach * allowed[ga, gb, g]
        limit = jnp.where((cell >= starts[g]) & (cell < starts[g] + counts[g]), reach, limit)
    bound[...] = limit
    own, width = denom.shape
    slot = column * width + lax.broadcasted_iota(jnp.int32, (own, width), 1)
    line = lax.broadcasted_iota(jnp.int32, (own, width), 0)
    first = start_b + column * width

    def put(s, acc):
        orb = first + s
        value = jnp.where(orb < total, vir_e[jnp.minimum(orb, total - 1)], 0.0)
        return jnp.where(slot == column * width + s, value, acc)

    eps_b = lax.fori_loop(0, width, put, jnp.zeros((own, width), F32), unroll=8)
    eps_ij = jnp.zeros((own, width), F32)
    for p in range(own):
        i, j = pair_list[0, y * own + p], pair_list[1, y * own + p]
        eps_ij = jnp.where(line == p, occ_e[i] + occ_e[j], eps_ij)
    denom[...] = eps_ij - vir_e[a_orb] - eps_b
    live[...] = (slot < count_b).astype(jnp.int32)


READY = 4
SLOTS = 4
PARTS = 4


def ready_body(*refs):
    slab = refs[8]
    out, bound, denom, live, held, sems = refs[-6:]
    width, cells, slots = slab.shape
    steps = cells // (8 * READY)
    share = width // PARTS

    def copies(s):
        return [
            pltpu.make_async_copy(
                slab.at[pl.ds(n * share, share), pl.ds(s * READY * 8, READY * 8), :],
                held.at[s % SLOTS, pl.ds(n * share, share)],
                sems.at[s % SLOTS, n],
            )
            for n in range(PARTS)
        ]

    for s in range(SLOTS - 1):
        for c in copies(s):
            c.start()
    labels(*refs[:8], bound, denom, live)
    for s in range(steps):
        if s + SLOTS - 1 < steps:
            for c in copies(s + SLOTS - 1):
                c.start()
        for c in copies(s):
            c.wait()
        for g in range(READY):
            block = held[s % SLOTS, :, 8 * g : 8 * g + 8, :].reshape(width // 2, 2, 8, slots)
            even, odd = block[:, 0], block[:, 1]
            first = lax.broadcasted_iota(jnp.int32, even.shape, 1) < CELLS
            lower_cells = jnp.where(first, even, pltpu.roll(odd, CELLS, 1)).reshape(width * CELLS, slots)
            upper_cells = jnp.where(first, pltpu.roll(even, CELLS, 1), odd).reshape(width * CELLS, slots)
            for i, rows in enumerate((lower_cells, upper_cells)):
                at = (s * READY + g) * 2 + i
                high, low = split(rows)
                out[at, pl.ds(0, width * CELLS)] = high
                out[at, pl.ds(width * CELLS, width * CELLS)] = low


def ready(place, tables, vir_tile, slab, own, pairs, after):
    width, cells, slots = slab.shape
    return pl.pallas_call(
        ready_body,
        out_shape=(
            jax.ShapeDtypeStruct((cells // CELLS, 2 * CELLS * width, slots), BF16),
            jax.ShapeDtypeStruct((cells // CELLS, CELLS * pairs), jnp.int32),
            jax.ShapeDtypeStruct((own, width), F32),
            jax.ShapeDtypeStruct((own, width), jnp.int32),
        ),
        in_specs=[smem()] * 7 + [vmem()] + [anywhere()] * (1 + len(after)),
        out_specs=(vmem(),) * 4,
        scratch_shapes=[
            pltpu.VMEM((SLOTS, width, READY * 8, slots), F32),
            pltpu.SemaphoreType.DMA((SLOTS, PARTS)),
        ],
        compiler_params=grant(28),
        cost_estimate=small_cost(),
    )(place, *(in_hbm(v) for v in tables), vir_tile, in_hbm(slab), *after)


STEP = 16


def ladder_body(last, base, place, bound, slab, mine, other, before, after, *rest):
    if last:
        parts, rest = rest[:4], rest[4:]
        o0, o1, o2, o3, amps, acc, folded, final = rest
    else:
        out, amps, acc, folded, final = rest
    y, core = place[0], place[3]
    _, rows, slots = slab.shape
    lanes = bound.shape[1]
    width = rows // (2 * CELLS)
    pairs = lanes // CELLS
    x, z = place[1], place[2]
    tiles = []
    for source, at_first in ((mine, core == 0), (other, core == 1)):
        for n, shift in enumerate((0, 3, 1, 2)):
            first = jnp.where(at_first, lax.rem(z + shift, 4) * 2, lax.rem(x + shift, 4) * 8 + 1)
            for i in range(4):
                tiles.append((source, 4 * n + i, first + i * jnp.where(at_first, 8, 2)))
    t_of = lax.broadcasted_iota(jnp.int32, (slots, lanes), 0)
    for s in range(mine.shape[0] // STEP):
        left, right = [], []
        for g in range(STEP):
            for source, n, tile in tiles:
                amps[g, tile] = source[s * STEP + g, n]
            at = base + s * STEP + g
            edge = bound[at : at + 1, :]
            high, low = split(jnp.where(t_of < edge, amps[g].reshape(slots, lanes), 0.0))
            left.append(slab[at])
            right.append(jnp.concatenate([high, low], axis=1))
        part = jnp.dot(jnp.concatenate(left, axis=1), jnp.concatenate(right, axis=0), preferred_element_type=F32)
        if s == 0:
            acc[...] = part
        else:
            acc[...] += part
    half = rows // 2
    folded[...] = (acc[:half, :lanes] + acc[:half, lanes:]) + (acc[half:, :lanes] + acc[half:, lanes:])
    total = jnp.zeros((width, pairs), F32)
    for j in range(CELLS):
        total = total + folded[pl.ds(j, width, stride=CELLS), :][:, j * pairs : (j + 1) * pairs]
    total = total.T
    if not last:
        out[...] = total if base == 0 else total + before[...]
        return
    if base:
        total = total + before[...]
    final[...] = total + (parts[0][...] + parts[1][...]) + (parts[2][...] + parts[3][...])
    own = pairs // 4
    for o, shift in ((o0, 0), (o1, 1), (o2, 3), (o3, 2)):
        o[...] = final[pl.ds(pl.multiple_of(lax.rem(y + shift, 4) * own, 8), own), :]


def ladder(place, bound, slab, mine, other, base, before, after, parts=()):
    last = bool(parts)
    _, rows, slots = slab.shape
    lanes = bound.shape[1]
    pairs = lanes // CELLS
    width = rows // (2 * CELLS)
    if last:
        out_shape = (jax.ShapeDtypeStruct((pairs // 4, width), F32),) * 4
        out_specs = (vmem(),) * 4
    else:
        out_shape = jax.ShapeDtypeStruct((pairs, width), F32)
        out_specs = vmem()
    return pl.pallas_call(
        functools.partial(ladder_body, last, base),
        out_shape=out_shape,
        in_specs=[smem()] + [vmem()] * 5 + [anywhere()] + [vmem()] * len(parts),
        out_specs=out_specs,
        scratch_shapes=[
            pltpu.VMEM((STEP, slots // 8, 8, lanes), F32),
            pltpu.VMEM((rows, 2 * lanes), F32),
            pltpu.VMEM((rows // 2, lanes), F32),
            pltpu.VMEM((pairs, width), F32),
        ],
        compiler_params=grant(12),
        cost_estimate=small_cost(),
    )(place, bound, in_vmem(slab), mine, other, before, after, *parts)


def on_device(vir, occ, allowed, pair_list, occ_e, vir_e, ladder_amp, int_slab, cycle_amp, cycle_int):
    row, column = lax.axis_index("row"), lax.axis_index("column")
    place = jnp.stack(
        [lax.axis_index("depth"), row // 2, (row % 2) * 2 + column // 2, column % 2]
    ).astype(jnp.int32)
    pairs = ladder_amp.shape[0]
    width = int_slab.shape[1]
    own = pairs // 4

    mine = relayout(jnp.transpose(ladder_amp, (0, 2, 1)))
    blocks = [mine] + [send(mine, FIRST[n]) for n in (1, -1, 2)]
    choice = (pair_list[:, 1:] == jnp.arange(cycle_int.shape[1], dtype=jnp.int32)).astype(F32)
    choice = jnp.repeat(choice, cycle_amp.shape[1], axis=0)
    share = cycle(place, cycle_amp, jnp.transpose(cycle_int, (1, 2, 0)), choice)
    low, high = stack(place, blocks, share)
    low_below, high_above = send(low, SECOND[1]), send(high, SECOND[-1])
    high_below, low_above = send(high, SECOND[1]), send(low, SECOND[-1])
    slab, bound, denom, live = ready(
        place,
        (vir, occ, allowed, pair_list.T, occ_e, vir_e),
        vir.reshape(8, -1),
        int_slab.reshape(int_slab.shape[1:]),
        own,
        pairs,
        (low_below, high_above),
    )
    held = [
        (low, low_below, low_above, send(low_below, SECOND[1])),
        (high, high_below, high_above, send(high_above, SECOND[-1])),
    ]
    *chunks, p0, p1, p2, p3 = pack(place, held, pairs, width, (bound,))
    others = [send(v, SWAP) for v in chunks]
    parts = spread((p0, p1, p2, p3), FIRST)
    sums = ladder(place, bound, slab, chunks[0], others[0], 0, bound, bound)
    sums = ladder(place, bound, slab, chunks[1], others[1], CHUNKS[0], sums, bound, parts)
    s0, s1, s2, s3 = spread(sums, ALONG_Y)
    total = (s0 + s1) + (s2 + s3)
    return jnp.where(live > 0, total / denom, jnp.float32(0.0))[None]


def solution(mesh):
    return jax.shard_map(
        on_device,
        mesh=mesh,
        in_specs=(
            P(),
            P(),
            P(),
            P(),
            P(),
            P(),
            P(None, "depth", ("row", "column")),
            P("row", "column", "depth", None),
            P(None, None, ("depth", "row")),
            P(("depth", "row"), None, "column"),
        ),
        out_specs=P("row", "depth", "column"),
        check_vma=False,
    )
```
